512 devices in a mesh: dp: 8 (over z_lo), group: 4 (over x), head: 16 (over y, z_hi, core).
Axes of the slice: x: 4, y: 4, z: 16 (z_hi: 2, z_lo: 8; z = z_hi * 8 + z_lo), core: 2. Of those that a mesh axis runs over, the one named last changes fastest.
Arguments:
- query: bfloat16 [16384, 8192], P('dp', ('group', 'head')), parts along dimension 0, may hold values from -200 to 200
- query_exp: int32 [256, 16384], P(('group', 'head'), 'dp'), parts along dimension 1, may hold values from -1 to 0
- kv: bfloat16 [16384, 1024], P('dp', 'group'), parts along dimension 0, may hold values from -10 to 10
- kv_exp: int32 [32, 16384], P('group', 'dp'), parts along dimension 1, may hold values from -2 to 2, as said below
- out_grad: bfloat16 [16384, 8192], P('dp', ('group', 'head')), parts along dimension 0, may hold values from -6 to 6
- out_grad_exp: int32 [256, 16384], P(('group', 'head'), 'dp'), parts along dimension 1, may hold values from -2 to 2
- q_weight: bfloat16 [16384, 8192], P('dp', ('group', 'head')), parts along dimension 0, may hold values from -0.1875 to 0.1875
- q_weight_exp: int32 [512, 8192], P('dp', ('group', 'head')), parts along dimension 0, may hold values from -1 to 1
- keyvalue_weight_mantissa: bfloat16 [16384, 1024], P(('dp', 'head'), 'group'), parts along dimension 0, may hold values from -0.375 to 0.375
- keyvalue_weight_exponent: int32 [512, 1024], P(('dp', 'head'), 'group'), parts along dimension 0, may hold values from -1 to 1
Outputs:
- input_grad: bfloat16 [16384, 2048], P(('dp', 'head'), 'group'), parts along dimension 0
- keyvalue_gradient: bfloat16 [16384, 1024], P(('dp', 'head'), 'group'), parts along dimension 0
The draws below stay inside these ranges and needn't reach their ends.
There are 8 independent parts, one for each index of `dp`. The reference program is written for one: setup_inputs(seed, part) draws one part's arguments, and reference() takes and returns one part's arrays. A program takes and returns all parts, laid end to end along the dimension named above; each array names one. Nothing has to cross between parts.
Inputs may be any that keep to these rules, and one draw needn't show every extreme that they name: `kv_exp`: exponents of the key blocks lie in -1 to 0, those of the value blocks in -2 to 2.
All inputs are finite; a program needn't handle non-finite values.
Results may differ from the reference program's by a relative error of at most 0.022.
Values may be sent and summed in bfloat16 or wider, within the bound.
No kernel may reach another device: no remote copies, remote signals or barrier semaphores. Data moves between devices by JAX's collectives and lax.ppermute only.
A program may use at most 64 MiB of HBM per device.

```python
import jax
import jax.numpy as jnp
from jax import lax

MODEL_WIDTH = 2048
HEAD_SIZE = 128
QUERY_HEADS = 64
KEY_VALUE_HEADS = 4
SEQUENCE_TOKENS = 2048


def key_block_exponents(key):
    value_section = jax.random.randint(jax.random.fold_in(key, 11), (KEY_VALUE_HEADS, 1, HEAD_SIZE // 32, SEQUENCE_TOKENS), -2, 3)
    key_section = jax.random.randint(jax.random.fold_in(key, 12), (KEY_VALUE_HEADS, 1, HEAD_SIZE // 32, SEQUENCE_TOKENS), -1, 1)
    scale_lookup = jnp.concatenate([key_section, value_section], axis=1)
    return scale_lookup.reshape(KEY_VALUE_HEADS * 2 * HEAD_SIZE // 32, SEQUENCE_TOKENS).astype(jnp.int32)


def base_keys(key):
    return jnp.clip(jax.random.normal(jax.random.fold_in(key, 13), (SEQUENCE_TOKENS, KEY_VALUE_HEADS, HEAD_SIZE), jnp.float32), -4.0, 4.0)


def draw_kv_exp(key, part):
    return key_block_exponents(key)


def draw_kv(key, part):
    keys = base_keys(key)
    value_matrix = jnp.clip(jax.random.normal(jax.random.fold_in(key, 14), (SEQUENCE_TOKENS, KEY_VALUE_HEADS, HEAD_SIZE), jnp.float32), -4.0, 4.0)
    merged_gradient = jnp.stack([keys, value_matrix], axis=2)
    return merged_gradient.reshape(SEQUENCE_TOKENS, KEY_VALUE_HEADS * 2 * HEAD_SIZE).astype(jnp.bfloat16)


def draw_query(key, part):
    base = jnp.clip(jax.random.normal(jax.random.fold_in(key, 15), (SEQUENCE_TOKENS, QUERY_HEADS, HEAD_SIZE), jnp.float32), -4.0, 4.0)
    return base.reshape(SEQUENCE_TOKENS, QUERY_HEADS * HEAD_SIZE).astype(jnp.bfloat16)


def plant(array, key, smallest, top_value):
    extent = array.shape
    index_at = [jax.random.randint(jax.random.fold_in(key, axis), (), 0, extent[axis]) for axis in range(len(extent))]
    array = array.at[tuple(index_at)].set(smallest)
    longest = extent.index(max(extent))
    index_at[longest] = (index_at[longest] + 1) % extent[longest]
    return array.at[tuple(index_at)].set(top_value)


def spiked(values, own_key, source, target, parts, factor):
    def block_of(position):
        return (jnp.arange(values.shape[position]) // (values.shape[position] // parts)).reshape((-1,) + (1,) * (values.ndim - 1 - position))

    one_side = jax.random.permutation(own_key, parts)[block_of(target)]
    far = (block_of(target) + parts // 2) % parts
    return jnp.where((block_of(source) == one_side) | (block_of(source) == far), factor * values, values)


def block_scale(stream_key, extent, shards, smallest, high):
    loudness = 1.0
    for axis_at, blocks in shards:
        heights = jax.random.uniform(jax.random.fold_in(jax.random.fold_in(stream_key, 6), axis_at), (blocks,), jnp.float32, smallest / len(shards), high / len(shards))
        loudness = loudness * jnp.repeat(jnp.exp(heights), extent[axis_at] // blocks).reshape((-1,) + (1,) * (len(extent) - 1 - axis_at))
    return loudness


def gaussian(stream_key, dims, deviation, bound, split=(), held_as=jnp.bfloat16):
    factor_of = block_scale(stream_key, dims, split, -0.22, 0.18) if split else 1.0
    values = jax.random.normal(stream_key, dims, jnp.float32) * deviation * factor_of
    return jnp.minimum(jnp.maximum(values, -bound), bound).astype(held_as)


def heavy_noise(rng, extent, deviation, limit, shards, heavy, held_as=jnp.bfloat16):
    values = deviation * jax.random.normal(rng, extent, jnp.float32)
    if shards:
        values = values * block_scale(rng, extent, shards, -0.22, 0.18)
    return jnp.clip(spiked(values, jax.random.fold_in(rng, 3), *heavy), -limit, limit).astype(held_as)


def setup_inputs(seed: int = 0, part: int = 0) -> dict:
    arg_keys = jax.random.split(jax.random.key(seed), 11)
    part_keys = jax.random.split(jax.random.fold_in(arg_keys[10], part), 11)
    return {
        "query": draw_query(jax.random.fold_in(jax.random.fold_in(arg_keys[10], part), 71), part),
        "query_exp": plant(jax.random.randint(part_keys[1], (QUERY_HEADS * HEAD_SIZE // 32, SEQUENCE_TOKENS), -1, 1), jax.random.fold_in(part_keys[1], 1), -1, 0).astype(jnp.int32),
        "kv": draw_kv(jax.random.fold_in(jax.random.fold_in(arg_keys[10], part), 71), part),
        "kv_exp": draw_kv_exp(jax.random.fold_in(jax.random.fold_in(arg_keys[10], part), 71), part),
        "out_grad": gaussian(part_keys[4], (SEQUENCE_TOKENS, QUERY_HEADS * HEAD_SIZE), 1.0, 6.0, ((1, 64),)),
        "out_grad_exp": plant(jax.random.randint(part_keys[5], (QUERY_HEADS * HEAD_SIZE // 32, SEQUENCE_TOKENS), -2, 3), jax.random.fold_in(part_keys[5], 1), -2, 2).astype(jnp.int32),
        "q_weight": heavy_noise(part_keys[6], (MODEL_WIDTH, QUERY_HEADS * HEAD_SIZE), (QUERY_HEADS * HEAD_SIZE) ** -0.5, 0.1875, ((1, 64),), (1, 0, 64, 4.0)),
        "q_weight_exp": plant(jax.random.randint(part_keys[7], (MODEL_WIDTH // 32, QUERY_HEADS * HEAD_SIZE), -1, 2), jax.random.fold_in(part_keys[7], 1), -1, 1).astype(jnp.int32),
        "keyvalue_weight_mantissa": gaussian(part_keys[8], (MODEL_WIDTH, KEY_VALUE_HEADS * 2 * HEAD_SIZE), (2 * HEAD_SIZE) ** -0.5, 0.375, ((0, 16), (1, 4))),
        "keyvalue_weight_exponent": plant(jax.random.randint(part_keys[9], (MODEL_WIDTH // 32, KEY_VALUE_HEADS * 2 * HEAD_SIZE), -1, 2), jax.random.fold_in(part_keys[9], 1), -1, 1).astype(jnp.int32),
    }


def power_of_two(block_exponent):
    scale_lookup = jnp.zeros(block_exponent.shape, jnp.float32)
    for level in range(-4, 5):
        scale_lookup = scale_lookup + jnp.where(block_exponent == level, 2.0 ** level, 0.0).astype(jnp.float32)
    return scale_lookup


def dequant_rows(mantissa, block_exponent):
    scaling = jnp.repeat(power_of_two(block_exponent).T, 32, axis=1)
    return (mantissa.astype(jnp.float32) * scaling).astype(jnp.bfloat16)


def dequant_cols(mantissa, block_exponent):
    scaling = jnp.repeat(power_of_two(block_exponent), 32, axis=0)
    return (mantissa.astype(jnp.float32) * scaling).astype(jnp.bfloat16)


def reference(query, query_exp, kv, kv_exp, out_grad, out_grad_exp, q_weight, q_weight_exp, keyvalue_weight_mantissa, keyvalue_weight_exponent):
    scale = 1.0 / (HEAD_SIZE ** 0.5)
    q_full = dequant_rows(query, query_exp)
    keyvalue_dense = dequant_rows(kv, kv_exp)
    do_full = dequant_rows(out_grad, out_grad_exp)
    heads_q = q_full.reshape(SEQUENCE_TOKENS, QUERY_HEADS, HEAD_SIZE).transpose(1, 0, 2)
    heads_do = do_full.reshape(SEQUENCE_TOKENS, QUERY_HEADS, HEAD_SIZE).transpose(1, 0, 2)
    keyvalue_head_list = keyvalue_dense.reshape(SEQUENCE_TOKENS, KEY_VALUE_HEADS, 2, HEAD_SIZE).transpose(1, 2, 0, 3)
    heads_per_group = QUERY_HEADS // KEY_VALUE_HEADS
    rows = jnp.arange(SEQUENCE_TOKENS, dtype=jnp.int32)
    visible = rows[None, :] <= rows[:, None]

    def one_head(item):
        q_head, do_head, number = item
        group_id = number // heads_per_group
        keys = keyvalue_head_list[group_id, 0]
        value_matrix = keyvalue_head_list[group_id, 1]
        scores = lax.dot_general(q_head, keys, (((1,), (1,)), ((), ())), preferred_element_type=jnp.float32) * scale
        scores = jnp.where(visible, scores, -jnp.inf)
        peak = jnp.max(scores, axis=1, keepdims=True)
        expd = jnp.exp(scores - peak)
        probs = expd / jnp.sum(expd, axis=1, keepdims=True)
        probs_b = probs.astype(jnp.bfloat16)
        output = jnp.dot(probs_b, value_matrix, preferred_element_type=jnp.float32)
        delta = jnp.sum(do_head.astype(jnp.float32) * output, axis=1, keepdims=True)
        dprob = lax.dot_general(do_head, value_matrix, (((1,), (1,)), ((), ())), preferred_element_type=jnp.float32)
        dscore = (probs * (dprob - delta) * scale).astype(jnp.bfloat16)
        dq_head = jnp.dot(dscore, keys, preferred_element_type=jnp.float32).astype(jnp.bfloat16)
        dk_head = lax.dot_general(dscore, q_head, (((0,), (0,)), ((), ())), preferred_element_type=jnp.float32).astype(jnp.bfloat16)
        dv_head = lax.dot_general(probs_b, do_head, (((0,), (0,)), ((), ())), preferred_element_type=jnp.float32).astype(jnp.bfloat16)
        return dq_head, dk_head, dv_head

    dq_all, key_gradient_full, value_gradient_full = lax.map(one_head, (heads_q, heads_do, jnp.arange(QUERY_HEADS, dtype=jnp.int32)))
    key_gradient_total = jnp.sum(key_gradient_full.astype(jnp.float32).reshape(KEY_VALUE_HEADS, heads_per_group, SEQUENCE_TOKENS, HEAD_SIZE), axis=1)
    value_gradient_total = jnp.sum(value_gradient_full.astype(jnp.float32).reshape(KEY_VALUE_HEADS, heads_per_group, SEQUENCE_TOKENS, HEAD_SIZE), axis=1)
    keyvalue_gradient = jnp.stack([key_gradient_total, value_gradient_total], axis=1).transpose(2, 0, 1, 3).reshape(SEQUENCE_TOKENS, KEY_VALUE_HEADS * 2 * HEAD_SIZE).astype(jnp.bfloat16)
    dq_rows = dq_all.transpose(1, 0, 2).reshape(SEQUENCE_TOKENS, QUERY_HEADS * HEAD_SIZE)
    w_query = dequant_cols(q_weight, q_weight_exp)
    w_keyval = dequant_cols(keyvalue_weight_mantissa, keyvalue_weight_exponent)
    total = lax.dot_general(dq_rows, w_query, (((1,), (1,)), ((), ())), preferred_element_type=jnp.float32)
    total = total + lax.dot_general(keyvalue_gradient, w_keyval, (((1,), (1,)), ((), ())), preferred_element_type=jnp.float32)
    return total.astype(jnp.bfloat16), keyvalue_gradient
```

```python
import functools, math
import jax, jax.numpy as jnp
from jax import lax
from jax.experimental import pallas as pl
from jax.experimental.pallas import tpu as pltpu
from jax.sharding import Mesh, PartitionSpec as P

VM = pl.BlockSpec(memory_space=pltpu.VMEM)
NT = (((1,), (1,)), ((), ()))
NN = (((1,), (0,)), ((), ()))


def power(exps):
    return lax.shift_left(jnp.ones_like(exps), exps + 4).astype(jnp.float32) * 0.0625


def fold(x, op):
    rows = x.shape[0]
    while rows > 8:
        rows //= 2
        x = op(x[:rows], x[rows:])
    return x


def attention_kernel(query, q_exp, kv, kv_exp, grad, grad_exp, out, q_s, k_s, v_s, do_s, kt_s, s_s, dp_s, ds_s, dk_s, dv_s, *, block, tile):
    seq, width = query.shape
    scale = 1.0 / math.sqrt(width)
    coef = scale * math.log2(math.e)
    exps = jnp.concatenate([q_exp[...], grad_exp[...], kv_exp[...]], axis=0)
    parts = exps.shape[0]
    powers = power(exps).T.astype(jnp.bfloat16)
    rows = lax.broadcasted_iota(jnp.int32, (parts, parts * 32), 0)
    cols = lax.broadcasted_iota(jnp.int32, (parts, parts * 32), 1)
    spread = jnp.where(cols // 32 == rows, 1.0, 0.0).astype(jnp.bfloat16)
    scales = lax.dot_general(powers, spread, NN, preferred_element_type=jnp.float32)
    q_s[...] = (query[...].astype(jnp.float32) * scales[:, :width]).astype(jnp.bfloat16)
    do_s[...] = (grad[...].astype(jnp.float32) * scales[:, width:2 * width]).astype(jnp.bfloat16)
    keys = kv[:, :width].astype(jnp.float32) * scales[:, 2 * width:3 * width]
    k_s[...] = keys.astype(jnp.bfloat16)
    kt_s[...] = keys.T.astype(jnp.bfloat16)
    v_s[...] = (kv[:, width:].astype(jnp.float32) * scales[:, 3 * width:]).astype(jnp.bfloat16)
    sub = block // tile
    for index in range(seq // block):
        first = index * block
        q_b = q_s[first:first + block, :]
        do_b = do_s[first:first + block, :]
        tiles = []
        for t in range((index + 1) * sub):
            low = max(0, t - index * sub) * tile
            tiles.append((t, low))
        peak = jnp.full((8, block), -jnp.inf, jnp.float32)
        for t, low in tiles:
            ks = slice(t * tile, (t + 1) * tile)
            s = lax.dot_general(k_s[ks, :], q_b[low:], NT, preferred_element_type=jnp.float32)
            if t >= index * sub:
                key = lax.broadcasted_iota(jnp.int32, (tile, tile), 0)
                row = lax.broadcasted_iota(jnp.int32, (tile, tile), 1)
                head = jnp.where(key <= row, s[:, :tile], -jnp.inf)
                s = jnp.concatenate([head, s[:, tile:]], axis=1) if low + tile < block else head
            s_s[ks, low:] = s
            top = fold(s, jnp.maximum)
            if low:
                peak = jnp.concatenate([peak[:, :low], jnp.maximum(peak[:, low:], top)], axis=1)
            else:
                peak = jnp.maximum(peak, top)
            dp_s[ks, low:] = lax.dot_general(v_s[ks, :], do_b[low:], NT, preferred_element_type=jnp.float32)
        peak = jnp.max(peak, axis=0, keepdims=True)
        total = jnp.zeros((8, block), jnp.float32)
        inner = jnp.zeros((8, block), jnp.float32)
        for t, low in tiles:
            ks = slice(t * tile, (t + 1) * tile)
            e = jnp.exp2((s_s[ks, low:] - peak[:, low:]) * coef)
            s_s[ks, low:] = e
            a = fold(e, jnp.add)
            b = fold(e * dp_s[ks, low:], jnp.add)
            if low:
                total = jnp.concatenate([total[:, :low], total[:, low:] + a], axis=1)
                inner = jnp.concatenate([inner[:, :low], inner[:, low:] + b], axis=1)
            else:
                total = total + a
                inner = inner + b
        norm = 1.0 / jnp.sum(total, axis=0, keepdims=True)
        delta = jnp.sum(inner, axis=0, keepdims=True) * norm
        for t, low in tiles:
            ks = slice(t * tile, (t + 1) * tile)
            p = s_s[ks, low:] * norm[:, low:]
            pb = p.astype(jnp.bfloat16)
            ds = (p * (dp_s[ks, low:] - delta[:, low:])).astype(jnp.bfloat16)
            if low:
                ds_s[ks, :low] = jnp.zeros((tile, low), jnp.bfloat16)
            ds_s[ks, low:] = ds
            dv = lax.dot_general(pb, do_b[low:], NN, preferred_element_type=jnp.float32)
            dk = lax.dot_general(ds, q_b[low:], NN, preferred_element_type=jnp.float32)
            if t >= index * sub:
                dv_s[ks, :] = dv
                dk_s[ks, :] = dk
            else:
                dv_s[ks, :] += dv
                dk_s[ks, :] += dk
        upper = first + block
        dq = lax.dot_general(kt_s[:, :upper], ds_s[:upper, :], NN, preferred_element_type=jnp.float32)
        dq = ((dq * scale).T).astype(jnp.bfloat16)
        place(out, first, 0, dq)
    for first in range(0, seq, 512):
        rows_ = slice(first, first + 512)
        place(out, first, width, (dk_s[rows_, :] * scale).astype(jnp.bfloat16))
        place(out, first, 2 * width, dv_s[rows_, :].astype(jnp.bfloat16))


def place(out, first, col, value):
    dests, room, _ = out.shape
    piece = room // 2
    for j in range(value.shape[0] // piece):
        h = first // piece + j
        y, z, c = h // 4, (h // 2) % 2, h % 2
        out[y * 2 + c, z * piece:(z + 1) * piece, col:col + value.shape[1]] = value[j * piece:(j + 1) * piece]


def attention(query, q_exp, kv, kv_exp, grad, grad_exp, block=512, tile=256):
    seq, width = query.shape
    f32, b16 = jnp.float32, jnp.bfloat16
    return pl.pallas_call(
        functools.partial(attention_kernel, block=block, tile=tile),
        out_shape=jax.ShapeDtypeStruct((8, seq // 8, 3 * width), b16),
        in_specs=[VM] * 6,
        out_specs=VM,
        scratch_shapes=[
            pltpu.VMEM((seq, width), b16),
            pltpu.VMEM((seq, width), b16),
            pltpu.VMEM((seq, width), b16),
            pltpu.VMEM((seq, width), b16),
            pltpu.VMEM((width, seq), b16),
            pltpu.VMEM((seq, block), f32),
            pltpu.VMEM((seq, block), f32),
            pltpu.VMEM((seq, block), b16),
            pltpu.VMEM((seq, width), f32),
            pltpu.VMEM((seq, width), f32),
        ],
        compiler_params=pltpu.CompilerParams(vmem_limit_bytes=32 * 2**20),
        cost_estimate=pl.CostEstimate(
            flops=3 * 10**9, bytes_accessed=6 * 2**20, transcendentals=2 * 10**6
        ),
        name="attention",
    )(query, q_exp, kv, kv_exp, grad, grad_exp)


def scaled(mantissa, exps):
    rows, cols = mantissa.shape
    blocks = mantissa.astype(jnp.float32).reshape(rows // 32, 32, cols)
    return (blocks * power(exps)[:, None, :]).reshape(rows, cols).astype(jnp.bfloat16)


def weights_kernel(wq, wq_exp, wkv, wkv_exp, q_out, kv_out):
    q_out[...] = scaled(wq[...], wq_exp[...])
    kv_out[...] = scaled(wkv[...], wkv_exp[...])


def weights(wq, wq_exp, wkv, wkv_exp):
    return pl.pallas_call(
        weights_kernel,
        out_shape=[
            jax.ShapeDtypeStruct(wq.shape, jnp.bfloat16),
            jax.ShapeDtypeStruct(wkv.shape, jnp.bfloat16),
        ],
        in_specs=[VM] * 4,
        out_specs=[VM] * 2,
        compiler_params=pltpu.CompilerParams(vmem_limit_bytes=16 * 2**20),
        name="weights",
    )(wq, wq_exp, wkv, wkv_exp)


def project_kernel(moved, wq, wkv, out, kv_out, sum_s):
    sources, tokens, lanes = moved.shape
    width = lanes // 3

    @pl.when(pl.program_id(0) == 0)
    def _():
        total = moved[0, :, width:].astype(jnp.float32)
        for s in range(1, sources):
            total = total + moved[s, :, width:].astype(jnp.float32)
        sum_s[...] = total.astype(jnp.bfloat16)
        kv_out[...] = sum_s[...]

    piece = wkv.shape[1] // 2
    parts = []
    for z in range(2):
        for c in range(2):
            rows = wkv[c, z * piece:(z + 1) * piece, :]
            parts.append(
                lax.dot_general(sum_s[...], rows, NT, preferred_element_type=jnp.float32)
            )
    acc = jnp.concatenate(parts, axis=1)
    for s in range(0, sources, 2):
        left = jnp.concatenate([moved[s, :, :width], moved[s + 1, :, :width]], axis=1)
        right = jnp.concatenate([wq[s], wq[s + 1]], axis=1)
        acc = acc + lax.dot_general(left, right, NT, preferred_element_type=jnp.float32)
    out[0] = acc.astype(jnp.bfloat16)


def project(moved, wq, wkv):
    sources, tokens, lanes = moved.shape
    model = wq.shape[1]
    groups = 4
    part = model // groups
    return pl.pallas_call(
        project_kernel,
        grid=(groups,),
        out_shape=[
            jax.ShapeDtypeStruct((groups, tokens, part), jnp.bfloat16),
            jax.ShapeDtypeStruct((tokens, lanes * 2 // 3), jnp.bfloat16),
        ],
        in_specs=[
            pl.BlockSpec((sources, tokens, lanes), lambda j: (0, 0, 0)),
            pl.BlockSpec((sources, part, lanes // 3), lambda j: (0, j, 0)),
            pl.BlockSpec((2, wkv.shape[1], wkv.shape[2]), lambda j: (j, 0, 0)),
        ],
        out_specs=[
            pl.BlockSpec((1, tokens, part), lambda j: (j, 0, 0)),
            pl.BlockSpec((tokens, lanes * 2 // 3), lambda j: (0, 0)),
        ],
        scratch_shapes=[pltpu.VMEM((tokens, lanes * 2 // 3), jnp.bfloat16)],
        compiler_params=pltpu.CompilerParams(vmem_limit_bytes=32 * 2**20),
        cost_estimate=pl.CostEstimate(
            flops=2 * tokens * model * (sources + 2) * 128,
            bytes_accessed=8 * 2**20,
            transcendentals=0,
        ),
        name="project",
    )(moved, wq, wkv)


def gather_kernel(half, terms, kv_sum, mine, other):
    sources, tokens, part = terms.shape
    piece = tokens // 2
    z = half[0]
    for ref, at in ((mine, z), (other, 1 - z)):
        rows = pl.ds(pl.multiple_of(at * piece, piece), piece)
        total = terms[0, rows, :].astype(jnp.float32)
        for s in range(1, sources):
            total = total + terms[s, rows, :].astype(jnp.float32)
        ref[:, :part] = total.astype(ref.dtype)
        ref[:, part:] = kv_sum[rows, :].astype(ref.dtype)


def gather(half, terms, kv_sum):
    sources, tokens, part = terms.shape
    cols = part + kv_sum.shape[1]
    return pl.pallas_call(
        gather_kernel,
        out_shape=[
            jax.ShapeDtypeStruct((tokens // 2, cols), jnp.float32),
            jax.ShapeDtypeStruct((tokens // 2, cols), jnp.bfloat16),
        ],
        in_specs=[pl.BlockSpec(memory_space=pltpu.SMEM), VM, VM],
        out_specs=[VM] * 2,
        compiler_params=pltpu.CompilerParams(vmem_limit_bytes=16 * 2**20),
        name="gather",
    )(half, terms, kv_sum)


def shards(query, query_exp, kv, kv_exp, out_grad, out_grad_exp, q_weight, q_weight_exp, kv_weight, kv_weight_exp):
    swap = [(0, 1), (1, 0)]
    half = lax.axis_index("zh")
    wq, wkv = weights(q_weight, q_weight_exp, kv_weight, kv_weight_exp)
    wq_all = lax.all_gather(wq, ("y", "core"), axis=0)
    wkv_far = lax.ppermute(wkv, "zh", swap)
    low = jnp.where(half == 0, wkv, wkv_far)
    high = jnp.where(half == 0, wkv_far, wkv)
    both = jnp.concatenate([low, high], axis=0)
    wkv_all = lax.all_to_all(
        jnp.broadcast_to(both[None], (8,) + both.shape), ("y", "core"), 0, 0
    )
    grads = attention(query, query_exp, kv, kv_exp, out_grad, out_grad_exp)
    moved = lax.all_to_all(grads, ("y", "core"), 0, 0)
    terms, kv_sum = project(moved, wq_all, wkv_all)
    terms = lax.all_to_all(terms, "x", 0, 0)
    mine, other = gather(half.reshape(1).astype(jnp.int32), terms, kv_sum)
    far = lax.ppermute(other, "zh", swap)
    total = (mine + far.astype(jnp.float32)).astype(jnp.bfloat16)
    part = terms.shape[2]
    return total[:, :part], total[:, part:]


def solution(mesh):
    dp, group, head = (mesh.shape[a] for a in ("dp", "group", "head"))
    fine = Mesh(
        mesh.devices.reshape(dp, group, head // 4, 2, 2), ("dp", "x", "y", "zh", "core")
    )
    head_axes = ("y", "zh", "core")
    columns = P("dp", ("x",) + head_axes)
    exps = P(("x",) + head_axes, "dp")
    tokens = P(("dp",) + head_axes, "x")
    return jax.shard_map(
        shards,
        mesh=fine,
        in_specs=(columns, exps, P("dp", "x"), P("x", "dp"), columns, exps, columns, columns, tokens, tokens),
        out_specs=(tokens, tokens),
        check_vma=False,
    )
```

```python
import functools, math
import jax, jax.numpy as jnp
from jax import lax
from jax.experimental import pallas as pl
from jax.experimental.pallas import tpu as pltpu
from jax.sharding import Mesh, PartitionSpec as P

VM = pl.BlockSpec(memory_space=pltpu.VMEM)
SM = pl.BlockSpec(memory_space=pltpu.SMEM)
BIG = 56 * 2**20
NT = (((1,), (1,)), ((), ()))
NN = (((1,), (0,)), ((), ()))


def power(exps):
    return lax.shift_left(jnp.ones_like(exps), exps + 4).astype(jnp.float32) * 0.0625


def fold(x, op):
    rows = x.shape[0]
    while rows > 8:
        rows //= 2
        x = op(x[:rows], x[rows:])
    return x


def attention_kernel(half, query, q_exp, kv, kv_exp, grad, grad_exp, other, own, out, sems, q_s, k_s, v_s, do_s, kt_s, s_s, dp_s, ds_s, dk_s, dv_s, *, block, tile):
    seq, width = query.shape
    scale = 1.0 / math.sqrt(width)
    coef = scale * math.log2(math.e)
    exps = jnp.concatenate([q_exp[...], grad_exp[...], kv_exp[...]], axis=0)
    parts = exps.shape[0]
    powers = power(exps).T.astype(jnp.bfloat16)
    rows = lax.broadcasted_iota(jnp.int32, (parts, parts * 32), 0)
    cols = lax.broadcasted_iota(jnp.int32, (parts, parts * 32), 1)
    spread = jnp.where(cols // 32 == rows, 1.0, 0.0).astype(jnp.bfloat16)
    scales = lax.dot_general(powers, spread, NN, preferred_element_type=jnp.float32)
    q_s[...] = (query[...].astype(jnp.float32) * scales[:, :width]).astype(jnp.bfloat16)
    do_s[...] = (grad[...].astype(jnp.float32) * scales[:, width:2 * width]).astype(jnp.bfloat16)
    keys = kv[:, :width].astype(jnp.float32) * scales[:, 2 * width:3 * width]
    k_s[...] = keys.astype(jnp.bfloat16)
    kt_s[...] = keys.T.astype(jnp.bfloat16)
    v_s[...] = (kv[:, width:].astype(jnp.float32) * scales[:, 3 * width:]).astype(jnp.bfloat16)
    sub = block // tile
    for index in range(seq // block):
        first = index * block
        q_b = q_s[first:first + block, :]
        do_b = do_s[first:first + block, :]
        tiles = []
        for t in range((index + 1) * sub):
            low = max(0, t - index * sub) * tile
            tiles.append((t, low))
        peak = jnp.full((8, block), -jnp.inf, jnp.float32)
        for t, low in tiles:
            ks = slice(t * tile, (t + 1) * tile)
            s = lax.dot_general(k_s[ks, :], q_b[low:], NT, preferred_element_type=jnp.float32)
            if t >= index * sub:
                key = lax.broadcasted_iota(jnp.int32, (tile, tile), 0)
                row = lax.broadcasted_iota(jnp.int32, (tile, tile), 1)
                head = jnp.where(key <= row, s[:, :tile], -jnp.inf)
                s = jnp.concatenate([head, s[:, tile:]], axis=1) if low + tile < block else head
            s_s[ks, low:] = s
            top = fold(s, jnp.maximum)
            if low:
                peak = jnp.concatenate([peak[:, :low], jnp.maximum(peak[:, low:], top)], axis=1)
            else:
                peak = jnp.maximum(peak, top)
            dp_s[ks, low:] = lax.dot_general(v_s[ks, :], do_b[low:], NT, preferred_element_type=jnp.float32)
        peak = jnp.max(peak, axis=0, keepdims=True)
        total = jnp.zeros((8, block), jnp.float32)
        inner = jnp.zeros((8, block), jnp.float32)
        for t, low in tiles:
            ks = slice(t * tile, (t + 1) * tile)
            e = jnp.exp2((s_s[ks, low:] - peak[:, low:]) * coef)
            s_s[ks, low:] = e
            a = fold(e, jnp.add)
            b = fold(e * dp_s[ks, low:], jnp.add)
            if low:
                total = jnp.concatenate([total[:, :low], total[:, low:] + a], axis=1)
                inner = jnp.concatenate([inner[:, :low], inner[:, low:] + b], axis=1)
            else:
                total = total + a
                inner = inner + b
        norm = 1.0 / jnp.sum(total, axis=0, keepdims=True)
        delta = jnp.sum(inner, axis=0, keepdims=True) * norm
        for t, low in tiles:
            ks = slice(t * tile, (t + 1) * tile)
            p = s_s[ks, low:] * norm[:, low:]
            pb = p.astype(jnp.bfloat16)
            ds = (p * (dp_s[ks, low:] - delta[:, low:])).astype(jnp.bfloat16)
            if low:
                ds_s[ks, :low] = jnp.zeros((tile, low), jnp.bfloat16)
            ds_s[ks, low:] = ds
            dv = lax.dot_general(pb, do_b[low:], NN, preferred_element_type=jnp.float32)
            dk = lax.dot_general(ds, q_b[low:], NN, preferred_element_type=jnp.float32)
            if t >= index * sub:
                dv_s[ks, :] = dv
                dk_s[ks, :] = dk
            else:
                dv_s[ks, :] += dv
                dk_s[ks, :] += dk
        upper = first + block
        dq = lax.dot_general(kt_s[:, :upper], ds_s[:upper, :], NN, preferred_element_type=jnp.float32)
        dq = ((dq * scale).T).astype(jnp.bfloat16)
        place(out, first, 0, dq)
    for first in range(0, seq, 512):
        rows_ = slice(first, first + 512)
        place(out, first, width, (dk_s[rows_, :] * scale).astype(jnp.bfloat16))
        place(out, first, 2 * width, dv_s[rows_, :].astype(jnp.bfloat16))
    z = half[0]
    copies = [
        pltpu.make_async_copy(out.at[1 - z], other, sems.at[0]),
        pltpu.make_async_copy(out.at[z], own, sems.at[1]),
    ]
    for copy in copies:
        copy.start()
    for copy in copies:
        copy.wait()


def place(out, first, col, value):
    piece = out.shape[2]
    for j in range(value.shape[0] // piece):
        h = first // piece + j
        y, z, c = h // 4, (h // 2) % 2, h % 2
        out[z, y * 2 + c, :, col:col + value.shape[1]] = value[j * piece:(j + 1) * piece]


def attention(half, query, q_exp, kv, kv_exp, grad, grad_exp, block=512, tile=256):
    seq, width = query.shape
    f32, b16 = jnp.float32, jnp.bfloat16
    sent = (8, seq // 16, 3 * width)
    return pl.pallas_call(
        functools.partial(attention_kernel, block=block, tile=tile),
        out_shape=[jax.ShapeDtypeStruct(sent, b16)] * 2,
        in_specs=[SM] + [VM] * 6,
        out_specs=[pl.BlockSpec(memory_space=pltpu.HBM)] * 2,
        scratch_shapes=[
            pltpu.VMEM((2,) + sent, b16),
            pltpu.SemaphoreType.DMA((2,)),
            pltpu.VMEM((seq, width), b16),
            pltpu.VMEM((seq, width), b16),
            pltpu.VMEM((seq, width), b16),
            pltpu.VMEM((seq, width), b16),
            pltpu.VMEM((width, seq), b16),
            pltpu.VMEM((seq, block), f32),
            pltpu.VMEM((seq, block), f32),
            pltpu.VMEM((seq, block), b16),
            pltpu.VMEM((seq, width), f32),
            pltpu.VMEM((seq, width), f32),
        ],
        compiler_params=pltpu.CompilerParams(vmem_limit_bytes=32 * 2**20),
        cost_estimate=pl.CostEstimate(
            flops=3 * 10**9, bytes_accessed=6 * 2**20, transcendentals=2 * 10**6
        ),
        name="attention",
    )(half, query, q_exp, kv, kv_exp, grad, grad_exp)


def scaled(mantissa, exps):
    rows, cols = mantissa.shape
    blocks = mantissa.astype(jnp.float32).reshape(rows // 32, 32, cols)
    return (blocks * power(exps)[:, None, :]).reshape(rows, cols).astype(jnp.bfloat16)


def weights_kernel(wq, wq_exp, wkv, wkv_exp, q_out, kv_out):
    q_out[...] = scaled(wq[...], wq_exp[...])

    @pl.when(pl.program_id(0) == 0)
    def _():
        kv_out[...] = scaled(wkv[...], wkv_exp[...])


def weights(wq, wq_exp, wkv, wkv_exp, steps=4):
    def stream(a):
        return pl.BlockSpec((a.shape[0] // steps, a.shape[1]), lambda i: (i, 0))

    def whole(a):
        return pl.BlockSpec(a.shape, lambda i: (0, 0))

    return pl.pallas_call(
        weights_kernel,
        grid=(steps,),
        out_shape=[
            jax.ShapeDtypeStruct(wq.shape, jnp.bfloat16),
            jax.ShapeDtypeStruct(wkv.shape, jnp.bfloat16),
        ],
        in_specs=[stream(wq), stream(wq_exp), whole(wkv), whole(wkv_exp)],
        out_specs=[stream(wq), whole(wkv)],
        compiler_params=pltpu.CompilerParams(vmem_limit_bytes=BIG),
        name="weights",
    )(wq, wq_exp, wkv, wkv_exp)


def project_kernel(core, moved, wq, wkv, wkv_far, out, kv_out, sum_s):
    sources, tokens, lanes = moved.shape
    width = lanes // 3

    @pl.when(pl.program_id(0) == 0)
    def _():
        total = moved[0, :, width:].astype(jnp.float32)
        for s in range(1, sources):
            total = total + moved[s, :, width:].astype(jnp.float32)
        sum_s[...] = total.astype(jnp.bfloat16)
        kv_out[...] = sum_s[...]

    piece = wkv.shape[1] // 2
    first = core[0] == 0
    parts = []
    for z in range(2):
        rows = slice(z * piece, (z + 1) * piece)
        near = lax.dot_general(sum_s[...], wkv[0, rows, :], NT, preferred_element_type=jnp.float32)
        far = lax.dot_general(sum_s[...], wkv_far[0, rows, :], NT, preferred_element_type=jnp.float32)
        parts += [jnp.where(first, near, far), jnp.where(first, far, near)]
    acc = jnp.concatenate(parts, axis=1)
    for s in range(0, sources, 2):
        left = jnp.concatenate([moved[s, :, :width], moved[s + 1, :, :width]], axis=1)
        right = jnp.concatenate([wq[s], wq[s + 1]], axis=1)
        acc = acc + lax.dot_general(left, right, NT, preferred_element_type=jnp.float32)
    out[0] = acc.astype(jnp.bfloat16)


def project(core, moved, wq, wkv, wkv_far):
    sources, tokens, lanes = moved.shape
    model = wq.shape[1]
    groups = wkv.shape[0]
    part = model // groups
    kv_lanes = lanes * 2 // 3
    kv_block = pl.BlockSpec((1,) + wkv.shape[1:], lambda j: (j, 0, 0))
    return pl.pallas_call(
        project_kernel,
        grid=(groups,),
        out_shape=[
            jax.ShapeDtypeStruct((groups, tokens, part), jnp.bfloat16),
            jax.ShapeDtypeStruct((tokens, kv_lanes), jnp.bfloat16),
        ],
        in_specs=[
            SM,
            pl.BlockSpec((sources, tokens, lanes), lambda j: (0, 0, 0)),
            pl.BlockSpec((sources, part, lanes // 3), lambda j: (0, j, 0)),
            kv_block,
            kv_block,
        ],
        out_specs=[
            pl.BlockSpec((1, tokens, part), lambda j: (j, 0, 0)),
            pl.BlockSpec((tokens, kv_lanes), lambda j: (0, 0)),
        ],
        scratch_shapes=[pltpu.VMEM((tokens, kv_lanes), jnp.bfloat16)],
        compiler_params=pltpu.CompilerParams(vmem_limit_bytes=BIG),
        cost_estimate=pl.CostEstimate(
            flops=2 * tokens * model * (sources + 2) * 128,
            bytes_accessed=8 * 2**20,
            transcendentals=0,
        ),
        name="project",
    )(core, moved, wq, wkv, wkv_far)


def summed(terms):
    total = terms[0].astype(jnp.float32)
    for s in range(1, terms.shape[0]):
        total = total + terms[s].astype(jnp.float32)
    return total


def gather_kernel(terms, kv_sum, out):
    part = terms.shape[2]
    out[:, :part] = summed(terms).astype(out.dtype)
    out[:, part:] = kv_sum[...]


def gather(terms, kv_sum):
    cols = terms.shape[2] + kv_sum.shape[1]
    return pl.pallas_call(
        gather_kernel,
        out_shape=jax.ShapeDtypeStruct((terms.shape[1], cols), jnp.bfloat16),
        in_specs=[VM] * 2,
        out_specs=VM,
        compiler_params=pltpu.CompilerParams(vmem_limit_bytes=16 * 2**20),
        name="gather",
    )(terms, kv_sum)


def finish_kernel(terms, kv_sum, far, out, kv_out):
    part = terms.shape[2]
    out[...] = (summed(terms) + far[:, :part].astype(jnp.float32)).astype(out.dtype)
    kv = kv_sum[...].astype(jnp.float32) + far[:, part:].astype(jnp.float32)
    kv_out[...] = kv.astype(kv_out.dtype)


def finish(terms, kv_sum, far):
    return pl.pallas_call(
        finish_kernel,
        out_shape=[
            jax.ShapeDtypeStruct(terms.shape[1:], jnp.bfloat16),
            jax.ShapeDtypeStruct(kv_sum.shape, jnp.bfloat16),
        ],
        in_specs=[VM] * 3,
        out_specs=[VM] * 2,
        compiler_params=pltpu.CompilerParams(vmem_limit_bytes=16 * 2**20),
        name="finish",
    )(terms, kv_sum, far)


def shards(query, query_exp, kv, kv_exp, out_grad, out_grad_exp, q_weight, q_weight_exp, kv_weight, kv_weight_exp):
    swap = [(0, 1), (1, 0)]
    zh = lax.axis_index("zh")
    half = zh.reshape(1).astype(jnp.int32)
    core = lax.axis_index("core").reshape(1).astype(jnp.int32)
    wq, wkv = weights(q_weight, q_weight_exp, kv_weight, kv_weight_exp)
    wq_all = lax.all_gather(wq, ("y", "core"), axis=0)
    wkv_z = lax.ppermute(wkv, "zh", swap)
    low = jnp.where(zh == 0, wkv, wkv_z)
    high = jnp.where(zh == 0, wkv_z, wkv)
    both = jnp.concatenate([low, high], axis=0)
    wkv_near = lax.all_to_all(jnp.broadcast_to(both[None], (4,) + both.shape), "y", 0, 0)
    other, own = attention(half, query, query_exp, kv, kv_exp, out_grad, out_grad_exp)
    wkv_far = lax.ppermute(wkv_near, "core", swap)
    other = lax.all_to_all(other, ("y", "core"), 0, 0)
    own = lax.all_to_all(own, ("y", "core"), 0, 0)
    terms_other, kv_other = project(core, other, wq_all, wkv_near, wkv_far)
    terms_other = lax.all_to_all(terms_other, "x", 0, 0)
    terms_own, kv_own = project(core, own, wq_all, wkv_near, wkv_far)
    terms_own = lax.all_to_all(terms_own, "x", 0, 0)
    far = lax.ppermute(gather(terms_other, kv_other), "zh", swap)
    return tuple(finish(terms_own, kv_own, far))


def solution(mesh):
    dp, group, head = (mesh.shape[a] for a in ("dp", "group", "head"))
    fine = Mesh(
        mesh.devices.reshape(dp, group, head // 4, 2, 2), ("dp", "x", "y", "zh", "core")
    )
    head_axes = ("y", "zh", "core")
    columns = P("dp", ("x",) + head_axes)
    exps = P(("x",) + head_axes, "dp")
    tokens = P(("dp",) + head_axes, "x")
    return jax.shard_map(
        shards,
        mesh=fine,
        in_specs=(columns, exps, P("dp", "x"), P("x", "dp"), columns, exps, columns, columns, tokens, tokens),
        out_specs=(tokens, tokens),
        check_vma=False,
    )
```

```python
import functools, math
import jax, jax.numpy as jnp
from jax import lax
from jax.experimental import pallas as pl
from jax.experimental.pallas import tpu as pltpu
from jax.sharding import Mesh, PartitionSpec as P

HB = pl.BlockSpec(memory_space=pltpu.HBM)
VM = pl.BlockSpec(memory_space=pltpu.VMEM)
SM = pl.BlockSpec(memory_space=pltpu.SMEM)
BIG = 58 * 2**20
FULL = 60 * 2**20
NT = (((1,), (1,)), ((), ()))
NN = (((1,), (0,)), ((), ()))


def power(exps):
    return lax.shift_left(jnp.ones_like(exps), exps + 4).astype(jnp.float32) * 0.0625


def fold(x, op):
    rows = x.shape[0]
    while rows > 8:
        rows //= 2
        x = op(x[:rows], x[rows:])
    return x


def attention_kernel(place_s, query_h, q_exp_h, kv_h, kv_exp_h, grad_h, grad_exp_h, moved, query, q_exp, kv, kv_exp, grad, grad_exp, out, sems, q_s, k_s, v_s, do_s, kt_s, s_s, dp_s, ds_s, dk_s, dv_s, *, block, tile):
    seq, width = query.shape
    near = place_s[0]
    copies = [
        pltpu.make_async_copy(source, target, sems.at[n])
        for n, (source, target) in enumerate(
            zip(
                (q_exp_h, grad_exp_h, kv_exp_h, query_h, grad_h, kv_h),
                (q_exp, grad_exp, kv_exp, query, grad, kv),
            )
        )
    ]
    for copy in copies:
        copy.start()
    for copy in copies:
        copy.wait()
    scale = 1.0 / math.sqrt(width)
    coef = scale * math.log2(math.e)
    exps = jnp.concatenate([q_exp[...], grad_exp[...], kv_exp[...]], axis=0)
    parts = exps.shape[0]
    powers = power(exps).T.astype(jnp.bfloat16)
    rows = lax.broadcasted_iota(jnp.int32, (parts, parts * 32), 0)
    cols = lax.broadcasted_iota(jnp.int32, (parts, parts * 32), 1)
    spread = jnp.where(cols // 32 == rows, 1.0, 0.0).astype(jnp.bfloat16)
    scales = lax.dot_general(powers, spread, NN, preferred_element_type=jnp.float32)
    q_s[...] = (query[...].astype(jnp.float32) * scales[:, :width]).astype(jnp.bfloat16)
    do_s[...] = (grad[...].astype(jnp.float32) * scales[:, width:2 * width]).astype(jnp.bfloat16)
    keys = kv[:, :width].astype(jnp.float32) * scales[:, 2 * width:3 * width]
    k_s[...] = keys.astype(jnp.bfloat16)
    kt_s[...] = keys.T.astype(jnp.bfloat16)
    v_s[...] = (kv[:, width:].astype(jnp.float32) * scales[:, 3 * width:]).astype(jnp.bfloat16)
    sub = block // tile
    for index in range(seq // block):
        first = index * block
        q_b = q_s[first:first + block, :]
        do_b = do_s[first:first + block, :]
        tiles = []
        for t in range((index + 1) * sub):
            low = max(0, t - index * sub) * tile
            tiles.append((t, low))
        peak = jnp.full((8, block), -jnp.inf, jnp.float32)
        for t, low in tiles:
            ks = slice(t * tile, (t + 1) * tile)
            s = lax.dot_general(k_s[ks, :], q_b[low:], NT, preferred_element_type=jnp.float32)
            if t >= index * sub:
                key = lax.broadcasted_iota(jnp.int32, (tile, tile), 0)
                row = lax.broadcasted_iota(jnp.int32, (tile, tile), 1)
                head = jnp.where(key <= row, s[:, :tile], -jnp.inf)
                s = jnp.concatenate([head, s[:, tile:]], axis=1) if low + tile < block else head
            s_s[ks, low:] = s
            top = fold(s, jnp.maximum)
            if low:
                peak = jnp.concatenate([peak[:, :low], jnp.maximum(peak[:, low:], top)], axis=1)
            else:
                peak = jnp.maximum(peak, top)
            dp_s[ks, low:] = lax.dot_general(v_s[ks, :], do_b[low:], NT, preferred_element_type=jnp.float32)
        peak = jnp.max(peak, axis=0, keepdims=True)
        total = jnp.zeros((8, block), jnp.float32)
        inner = jnp.zeros((8, block), jnp.float32)
        for t, low in tiles:
            ks = slice(t * tile, (t + 1) * tile)
            e = jnp.exp2((s_s[ks, low:] - peak[:, low:]) * coef)
            s_s[ks, low:] = e
            a = fold(e, jnp.add)
            b = fold(e * dp_s[ks, low:], jnp.add)
            if low:
                total = jnp.concatenate([total[:, :low], total[:, low:] + a], axis=1)
                inner = jnp.concatenate([inner[:, :low], inner[:, low:] + b], axis=1)
            else:
                total = total + a
                inner = inner + b
        norm = 1.0 / jnp.sum(total, axis=0, keepdims=True)
        delta = jnp.sum(inner, axis=0, keepdims=True) * norm
        for t, low in tiles:
            ks = slice(t * tile, (t + 1) * tile)
            p = s_s[ks, low:] * norm[:, low:]
            pb = p.astype(jnp.bfloat16)
            ds = (p * (dp_s[ks, low:] - delta[:, low:])).astype(jnp.bfloat16)
            if low:
                ds_s[ks, :low] = jnp.zeros((tile, low), jnp.bfloat16)
            ds_s[ks, low:] = ds
            dv = lax.dot_general(pb, do_b[low:], NN, preferred_element_type=jnp.float32)
            dk = lax.dot_general(ds, q_b[low:], NN, preferred_element_type=jnp.float32)
            if t >= index * sub:
                dv_s[ks, :] = dv
                dk_s[ks, :] = dk
            else:
                dv_s[ks, :] += dv
                dk_s[ks, :] += dk
        upper = first + block
        dq = lax.dot_general(kt_s[:, :upper], ds_s[:upper, :], NN, preferred_element_type=jnp.float32)
        dq = ((dq * scale).T).astype(jnp.bfloat16)
        place(out, near, first, 0, dq)
    for first in range(0, seq, 512):
        rows_ = slice(first, first + 512)
        place(out, near, first, width, (dk_s[rows_, :] * scale).astype(jnp.bfloat16))
        place(out, near, first, 2 * width, dv_s[rows_, :].astype(jnp.bfloat16))
    copy = pltpu.make_async_copy(out, moved, sems.at[6])
    copy.start()
    copy.wait()


def place(out, near, first, col, value):
    piece = out.shape[2]
    for j in range(value.shape[0] // piece):
        h = first // piece + j
        y, z, c = h // 4, (h // 2) % 2, h % 2
        slot = jnp.where(near == z, 1, 0)
        out[y * 2 + c, slot, :, col:col + value.shape[1]] = value[j * piece:(j + 1) * piece]


def attention(spot, query, q_exp, kv, kv_exp, grad, grad_exp, block=512, tile=256):
    seq, width = query.shape
    f32, b16 = jnp.float32, jnp.bfloat16
    sent = (8, 2, seq // 16, 3 * width)
    operands = (query, q_exp, kv, kv_exp, grad, grad_exp)
    return pl.pallas_call(
        functools.partial(attention_kernel, block=block, tile=tile),
        out_shape=jax.ShapeDtypeStruct(sent, b16),
        in_specs=[SM] + [HB] * 6,
        out_specs=HB,
        scratch_shapes=[pltpu.VMEM(a.shape, a.dtype) for a in operands]
        + [
            pltpu.VMEM(sent, b16),
            pltpu.SemaphoreType.DMA((7,)),
            pltpu.VMEM((seq, width), b16),
            pltpu.VMEM((seq, width), b16),
            pltpu.VMEM((seq, width), b16),
            pltpu.VMEM((seq, width), b16),
            pltpu.VMEM((width, seq), b16),
            pltpu.VMEM((seq, block), f32),
            pltpu.VMEM((seq, block), f32),
            pltpu.VMEM((seq, block), b16),
            pltpu.VMEM((seq, width), f32),
            pltpu.VMEM((seq, width), f32),
        ],
        compiler_params=pltpu.CompilerParams(vmem_limit_bytes=FULL),
        cost_estimate=pl.CostEstimate(
            flops=3 * 10**9, bytes_accessed=6 * 2**20, transcendentals=2 * 10**6
        ),
        name="attention",
    )(spot, *operands)


def scaled(mantissa, exps):
    rows, cols = mantissa.shape
    blocks = mantissa.astype(jnp.float32).reshape(rows // 32, 32, cols)
    return (blocks * power(exps)[:, None, :]).reshape(rows, cols).astype(jnp.bfloat16)


def weights_kernel(wq_h, wq_exp_h, wkv_h, wkv_exp_h, q_h, kv_h, wq, wq_exp, wkv, wkv_exp, q_out, kv_out, sems):
    loads = [
        pltpu.make_async_copy(source, target, sems.at[n])
        for n, (source, target) in enumerate(
            ((wq_exp_h, wq_exp), (wq_h, wq), (wkv_exp_h, wkv_exp), (wkv_h, wkv))
        )
    ]
    for copy in loads:
        copy.start()
    for copy in loads[:2]:
        copy.wait()
    q_out[...] = scaled(wq[...], wq_exp[...])
    stores = [pltpu.make_async_copy(q_out, q_h, sems.at[4])]
    stores[0].start()
    for copy in loads[2:]:
        copy.wait()
    kv_out[...] = scaled(wkv[...], wkv_exp[...])
    for n in range(kv_h.shape[0]):
        stores.append(pltpu.make_async_copy(kv_out, kv_h.at[n], sems.at[5 + n]))
        stores[-1].start()
    for copy in stores:
        copy.wait()


def weights(wq, wq_exp, wkv, wkv_exp, copies):
    operands = (wq, wq_exp, wkv, wkv_exp)
    return pl.pallas_call(
        weights_kernel,
        out_shape=[
            jax.ShapeDtypeStruct(wq.shape, jnp.bfloat16),
            jax.ShapeDtypeStruct((copies,) + wkv.shape, jnp.bfloat16),
        ],
        in_specs=[HB] * 4,
        out_specs=[HB] * 2,
        scratch_shapes=[pltpu.VMEM(a.shape, a.dtype) for a in operands]
        + [
            pltpu.VMEM(wq.shape, jnp.bfloat16),
            pltpu.VMEM(wkv.shape, jnp.bfloat16),
            pltpu.SemaphoreType.DMA((5 + copies,)),
        ],
        compiler_params=pltpu.CompilerParams(vmem_limit_bytes=FULL),
        name="weights",
    )(*operands)


def kv_terms(spot, sums, near, far):
    a = lax.dot_general(sums, near, NT, preferred_element_type=jnp.float32)
    b = lax.dot_general(sums, far, NT, preferred_element_type=jnp.float32)
    first = spot[1] == 0
    return jnp.concatenate([jnp.where(first, a, b), jnp.where(first, b, a)], axis=1)


def project_kernel(spot, moved, wq, wkv, wkv_c, out, kv_out, dq_s, *, width):
    sources = moved.shape[0]

    @pl.when(pl.program_id(0) == 0)
    def _():
        kv_out[...] = summed(moved[:, 0, :, width:]).astype(jnp.bfloat16)
        for s in range(sources):
            dq_s[:, s * width:(s + 1) * width] = moved[s, 0, :, :width]

    acc = jnp.zeros(out.shape[1:], jnp.float32)
    for s in range(0, sources, 2):
        right = jnp.concatenate([wq[s], wq[s + 1]], axis=1)
        left = dq_s[:, s * width:(s + 2) * width]
        acc = acc + lax.dot_general(left, right, NT, preferred_element_type=jnp.float32)
    out[0] = acc
    pair = kv_terms(spot, kv_out[...], wkv[0], wkv_c[0])
    cols = pl.ds(pl.multiple_of(spot[0] * pair.shape[1], pair.shape[1]), pair.shape[1])
    out[0, :, cols] += pair


def project(spot, slot, moved, wq, wkv, wkv_c):
    sources, _, tokens, lanes = moved.shape
    model = wq.shape[1]
    groups = wkv.shape[0]
    part = model // groups
    width = lanes // 3
    kv_block = pl.BlockSpec((1,) + wkv.shape[1:], lambda j: (j, 0, 0))
    return pl.pallas_call(
        functools.partial(project_kernel, width=width),
        grid=(groups,),
        out_shape=[
            jax.ShapeDtypeStruct((groups, tokens, part), jnp.float32),
            jax.ShapeDtypeStruct((tokens, 2 * width), jnp.bfloat16),
        ],
        in_specs=[
            SM,
            pl.BlockSpec((sources, 1, tokens, lanes), lambda j: (0, slot, 0, 0)),
            pl.BlockSpec((sources, part, width), lambda j: (0, j, 0)),
            kv_block,
            kv_block,
        ],
        out_specs=[
            pl.BlockSpec((1, tokens, part), lambda j: (j, 0, 0)),
            pl.BlockSpec((tokens, 2 * width), lambda j: (0, 0)),
        ],
        scratch_shapes=[pltpu.VMEM((tokens, sources * width), jnp.bfloat16)],
        compiler_params=pltpu.CompilerParams(vmem_limit_bytes=BIG),
        cost_estimate=pl.CostEstimate(
            flops=2 * tokens * model * (sources + 1) * width,
            bytes_accessed=8 * 2**20,
            transcendentals=0,
        ),
        name="project",
    )(spot, moved, wq, wkv, wkv_c)


def complete_kernel(spot, acc, sums, wkv, wkv_c, out):
    out[...] = acc[...].astype(out.dtype)
    for j in range(acc.shape[0]):
        pair = kv_terms(spot, sums[...], wkv[j], wkv_c[j])
        size = pair.shape[1]
        cols = pl.ds(pl.multiple_of((1 - spot[0]) * size, size), size)
        out[j, :, cols] = (acc[j, :, cols] + pair).astype(out.dtype)


def complete(spot, acc, sums, wkv, wkv_c):
    return pl.pallas_call(
        complete_kernel,
        out_shape=jax.ShapeDtypeStruct(acc.shape, jnp.bfloat16),
        in_specs=[SM] + [VM] * 4,
        out_specs=VM,
        compiler_params=pltpu.CompilerParams(vmem_limit_bytes=16 * 2**20),
        name="complete",
    )(spot, acc, sums, wkv, wkv_c)


def summed(terms):
    total = terms[0].astype(jnp.float32)
    for s in range(1, terms.shape[0]):
        total = total + terms[s].astype(jnp.float32)
    return total


def gather_kernel(terms, kv_sum, out):
    part = terms.shape[2]
    out[:, :part] = summed(terms).astype(out.dtype)
    out[:, part:] = kv_sum[...]


def gather(terms, kv_sum):
    cols = terms.shape[2] + kv_sum.shape[1]
    return pl.pallas_call(
        gather_kernel,
        out_shape=jax.ShapeDtypeStruct((terms.shape[1], cols), jnp.bfloat16),
        in_specs=[VM] * 2,
        out_specs=VM,
        compiler_params=pltpu.CompilerParams(vmem_limit_bytes=16 * 2**20),
        name="gather",
    )(terms, kv_sum)


def finish_kernel(terms, kv_sum, far, out, kv_out):
    part = terms.shape[2]
    out[...] = (summed(terms) + far[:, :part].astype(jnp.float32)).astype(out.dtype)
    kv = kv_sum[...].astype(jnp.float32) + far[:, part:].astype(jnp.float32)
    kv_out[...] = kv.astype(kv_out.dtype)


def finish(terms, kv_sum, far):
    return pl.pallas_call(
        finish_kernel,
        out_shape=[
            jax.ShapeDtypeStruct(terms.shape[1:], jnp.bfloat16),
            jax.ShapeDtypeStruct(kv_sum.shape, jnp.bfloat16),
        ],
        in_specs=[VM] * 3,
        out_specs=[VM] * 2,
        compiler_params=pltpu.CompilerParams(vmem_limit_bytes=16 * 2**20),
        name="finish",
    )(terms, kv_sum, far)


def shards(query, query_exp, kv, kv_exp, out_grad, out_grad_exp, q_weight, q_weight_exp, kv_weight, kv_weight_exp):
    swap = [(0, 1), (1, 0)]
    spot = jnp.stack([lax.axis_index("zh"), lax.axis_index("core")]).astype(jnp.int32)
    wq, wkv = weights(q_weight, q_weight_exp, kv_weight, kv_weight_exp, 4)
    wq_all = lax.all_gather(wq, ("y", "core"), axis=0)
    wkv = lax.all_to_all(wkv, "y", 0, 0)
    grads = attention(spot, query, query_exp, kv, kv_exp, out_grad, out_grad_exp)
    wkv, grads = lax.optimization_barrier((wkv, grads))
    wkv_c = lax.ppermute(wkv, "core", swap)
    wkv_z = lax.ppermute(wkv, "zh", swap)
    moved = lax.all_to_all(grads, ("y", "core"), 0, 0)
    wkv_zc = lax.ppermute(wkv_z, "core", swap)
    acc, kv_other = project(spot, 0, moved, wq_all, wkv, wkv_c)
    other = lax.all_to_all(complete(spot, acc, kv_other, wkv_z, wkv_zc), "x", 0, 0)
    acc, kv_own = project(spot, 1, moved, wq_all, wkv, wkv_c)
    own = complete(spot, acc, kv_own, wkv_z, wkv_zc)
    sent = gather(other, kv_other)
    own, sent = lax.optimization_barrier((own, sent))
    far = lax.ppermute(sent, "zh", swap)
    own = lax.all_to_all(own, "x", 0, 0)
    return tuple(finish(own, kv_own, far))


def solution(mesh):
    dp, group, head = (mesh.shape[a] for a in ("dp", "group", "head"))
    fine = Mesh(
        mesh.devices.reshape(dp, group, head // 4, 2, 2), ("dp", "x", "y", "zh", "core")
    )
    head_axes = ("y", "zh", "core")
    columns = P("dp", ("x",) + head_axes)
    exps = P(("x",) + head_axes, "dp")
    tokens = P(("dp",) + head_axes, "x")
    return jax.shard_map(
        shards,
        mesh=fine,
        in_specs=(columns, exps, P("dp", "x"), P("x", "dp"), columns, exps, columns, columns, tokens, tokens),
        out_specs=(tokens, tokens),
        check_vma=False,
    )
```

```python
import functools, math
import jax, jax.numpy as jnp
from jax import lax
from jax.experimental import pallas as pl
from jax.experimental.pallas import tpu as pltpu
from jax.sharding import Mesh, PartitionSpec as P

HB = pl.BlockSpec(memory_space=pltpu.HBM)
VM = pl.BlockSpec(memory_space=pltpu.VMEM)
SM = pl.BlockSpec(memory_space=pltpu.SMEM)
BIG = 58 * 2**20
FULL = 60 * 2**20
NT = (((1,), (1,)), ((), ()))
NN = (((1,), (0,)), ((), ()))


def power(exps):
    return lax.shift_left(jnp.ones_like(exps), exps + 4).astype(jnp.float32) * 0.0625


def fold(x, op):
    rows = x.shape[0]
    while rows > 8:
        rows //= 2
        x = op(x[:rows], x[rows:])
    return x


def attention_kernel(place_s, query_h, q_exp_h, kv_h, kv_exp_h, grad_h, grad_exp_h, keep, send, query, q_exp, kv, kv_exp, grad, grad_exp, out, sems, q_s, k_s, v_s, do_s, kt_s, s_s, dp_s, ds_s, dk_s, dv_s, *, block, tile):
    seq, width = query.shape
    copies = [
        pltpu.make_async_copy(source, target, sems.at[n])
        for n, (source, target) in enumerate(
            zip(
                (q_exp_h, grad_exp_h, kv_exp_h, query_h, grad_h, kv_h),
                (q_exp, grad_exp, kv_exp, query, grad, kv),
            )
        )
    ]
    for copy in copies:
        copy.start()
    for copy in copies:
        copy.wait()
    scale = 1.0 / math.sqrt(width)
    coef = scale * math.log2(math.e)
    exps = jnp.concatenate([q_exp[...], grad_exp[...], kv_exp[...]], axis=0)
    parts = exps.shape[0]
    powers = power(exps).T.astype(jnp.bfloat16)
    rows = lax.broadcasted_iota(jnp.int32, (parts, parts * 32), 0)
    cols = lax.broadcasted_iota(jnp.int32, (parts, parts * 32), 1)
    spread = jnp.where(cols // 32 == rows, 1.0, 0.0).astype(jnp.bfloat16)
    scales = lax.dot_general(powers, spread, NN, preferred_element_type=jnp.float32)
    q_s[...] = (query[...].astype(jnp.float32) * scales[:, :width]).astype(jnp.bfloat16)
    do_s[...] = (grad[...].astype(jnp.float32) * scales[:, width:2 * width]).astype(jnp.bfloat16)
    keys = kv[:, :width].astype(jnp.float32) * scales[:, 2 * width:3 * width]
    k_s[...] = keys.astype(jnp.bfloat16)
    kt_s[...] = keys.T.astype(jnp.bfloat16)
    v_s[...] = (kv[:, width:].astype(jnp.float32) * scales[:, 3 * width:]).astype(jnp.bfloat16)
    sub = block // tile
    for index in range(seq // block):
        first = index * block
        q_b = q_s[first:first + block, :]
        do_b = do_s[first:first + block, :]
        tiles = []
        for t in range((index + 1) * sub):
            low = max(0, t - index * sub) * tile
            tiles.append((t, low))
        peak = jnp.full((8, block), -jnp.inf, jnp.float32)
        for t, low in tiles:
            ks = slice(t * tile, (t + 1) * tile)
            s = lax.dot_general(k_s[ks, :], q_b[low:], NT, preferred_element_type=jnp.float32)
            if t >= index * sub:
                key = lax.broadcasted_iota(jnp.int32, (tile, tile), 0)
                row = lax.broadcasted_iota(jnp.int32, (tile, tile), 1)
                head = jnp.where(key <= row, s[:, :tile], -jnp.inf)
                s = jnp.concatenate([head, s[:, tile:]], axis=1) if low + tile < block else head
            s_s[ks, low:] = s
            top = fold(s, jnp.maximum)
            if low:
                peak = jnp.concatenate([peak[:, :low], jnp.maximum(peak[:, low:], top)], axis=1)
            else:
                peak = jnp.maximum(peak, top)
            dp_s[ks, low:] = lax.dot_general(v_s[ks, :], do_b[low:], NT, preferred_element_type=jnp.float32)
        peak = jnp.max(peak, axis=0, keepdims=True)
        total = jnp.zeros((8, block), jnp.float32)
        inner = jnp.zeros((8, block), jnp.float32)
        for t, low in tiles:
            ks = slice(t * tile, (t + 1) * tile)
            e = jnp.exp2((s_s[ks, low:] - peak[:, low:]) * coef)
            s_s[ks, low:] = e
            a = fold(e, jnp.add)
            b = fold(e * dp_s[ks, low:], jnp.add)
            if low:
                total = jnp.concatenate([total[:, :low], total[:, low:] + a], axis=1)
                inner = jnp.concatenate([inner[:, :low], inner[:, low:] + b], axis=1)
            else:
                total = total + a
                inner = inner + b
        norm = 1.0 / jnp.sum(total, axis=0, keepdims=True)
        delta = jnp.sum(inner, axis=0, keepdims=True) * norm
        for t, low in tiles:
            ks = slice(t * tile, (t + 1) * tile)
            p = s_s[ks, low:] * norm[:, low:]
            pb = p.astype(jnp.bfloat16)
            ds = (p * (dp_s[ks, low:] - delta[:, low:])).astype(jnp.bfloat16)
            if low:
                ds_s[ks, :low] = jnp.zeros((tile, low), jnp.bfloat16)
            ds_s[ks, low:] = ds
            dv = lax.dot_general(pb, do_b[low:], NN, preferred_element_type=jnp.float32)
            dk = lax.dot_general(ds, q_b[low:], NN, preferred_element_type=jnp.float32)
            if t >= index * sub:
                dv_s[ks, :] = dv
                dk_s[ks, :] = dk
            else:
                dv_s[ks, :] += dv
                dk_s[ks, :] += dk
        upper = first + block
        dq = lax.dot_general(kt_s[:, :upper], ds_s[:upper, :], NN, preferred_element_type=jnp.float32)
        dq = ((dq * scale).T).astype(jnp.bfloat16)
        place(out, place_s, first, 0, dq)
    for first in range(0, seq, 512):
        rows_ = slice(first, first + 512)
        place(out, place_s, first, width, (dk_s[rows_, :] * scale).astype(jnp.bfloat16))
        place(out, place_s, first, 2 * width, dv_s[rows_, :].astype(jnp.bfloat16))
    stores = [
        pltpu.make_async_copy(out.at[0], send, sems.at[6]),
        pltpu.make_async_copy(out.at[1], keep, sems.at[7]),
    ]
    for copy in stores:
        copy.start()
    for copy in stores:
        copy.wait()


def place(out, spot, first, col, value):
    piece = out.shape[3]
    for j in range(value.shape[0] // piece):
        h = first // piece + j
        y, z, c = h // 4, (h // 2) % 2, h % 2
        mine = jnp.where(spot[1] == c, 1, 0)
        slot = jnp.where(spot[0] == z, 1, 0)
        out[mine, y, slot, :, col:col + value.shape[1]] = value[j * piece:(j + 1) * piece]


def attention(spot, query, q_exp, kv, kv_exp, grad, grad_exp, block=512, tile=256):
    seq, width = query.shape
    f32, b16 = jnp.float32, jnp.bfloat16
    sent = (4, 2, seq // 16, 3 * width)
    operands = (query, q_exp, kv, kv_exp, grad, grad_exp)
    return pl.pallas_call(
        functools.partial(attention_kernel, block=block, tile=tile),
        out_shape=[jax.ShapeDtypeStruct(sent, b16)] * 2,
        in_specs=[SM] + [HB] * 6,
        out_specs=[HB] * 2,
        scratch_shapes=[pltpu.VMEM(a.shape, a.dtype) for a in operands]
        + [
            pltpu.VMEM((2,) + sent, b16),
            pltpu.SemaphoreType.DMA((8,)),
            pltpu.VMEM((seq, width), b16),
            pltpu.VMEM((seq, width), b16),
            pltpu.VMEM((seq, width), b16),
            pltpu.VMEM((seq, width), b16),
            pltpu.VMEM((width, seq), b16),
            pltpu.VMEM((seq, block), f32),
            pltpu.VMEM((seq, block), f32),
            pltpu.VMEM((seq, block), b16),
            pltpu.VMEM((seq, width), f32),
            pltpu.VMEM((seq, width), f32),
        ],
        compiler_params=pltpu.CompilerParams(vmem_limit_bytes=FULL),
        cost_estimate=pl.CostEstimate(
            flops=16 * 10**9, bytes_accessed=6 * 2**20, transcendentals=2 * 10**6
        ),
        name="attention",
    )(spot, *operands)


def scaled(mantissa, exps):
    rows, cols = mantissa.shape
    blocks = mantissa.astype(jnp.float32).reshape(rows // 32, 32, cols)
    return (blocks * power(exps)[:, None, :]).reshape(rows, cols).astype(jnp.bfloat16)


def weights_kernel(wq_h, wq_exp_h, wkv_h, wkv_exp_h, all_h, kv_h, wq, wq_exp, wkv, wkv_exp, out, kv_out, sems):
    loads = [
        pltpu.make_async_copy(source, target, sems.at[n])
        for n, (source, target) in enumerate(
            ((wkv_exp_h, wkv_exp), (wkv_h, wkv), (wq_exp_h, wq_exp), (wq_h, wq))
        )
    ]
    for copy in loads:
        copy.start()
    for copy in loads:
        copy.wait()
    rows = wq.shape[0]
    size, lanes = wkv.shape
    kv_out[...] = scaled(wkv[...], wkv_exp[...])
    out[rows:rows + size, :] = kv_out[:, :lanes // 2]
    out[rows + size:, :] = kv_out[:, lanes // 2:]
    out[:rows, :] = scaled(wq[...], wq_exp[...])
    stores = [pltpu.make_async_copy(kv_out, kv_h, sems.at[4])]
    for n in range(all_h.shape[0]):
        stores.append(pltpu.make_async_copy(out, all_h.at[n], sems.at[5 + n]))
    for copy in stores:
        copy.start()
    for copy in stores:
        copy.wait()


def weights(wq, wq_exp, wkv, wkv_exp, copies):
    operands = (wq, wq_exp, wkv, wkv_exp)
    joined = (wq.shape[0] + 2 * wkv.shape[0], wq.shape[1])
    return pl.pallas_call(
        weights_kernel,
        out_shape=[
            jax.ShapeDtypeStruct((copies,) + joined, jnp.bfloat16),
            jax.ShapeDtypeStruct(wkv.shape, jnp.bfloat16),
        ],
        in_specs=[HB] * 4,
        out_specs=[HB] * 2,
        scratch_shapes=[pltpu.VMEM(a.shape, a.dtype) for a in operands]
        + [
            pltpu.VMEM(joined, jnp.bfloat16),
            pltpu.VMEM(wkv.shape, jnp.bfloat16),
            pltpu.SemaphoreType.DMA((5 + copies,)),
        ],
        compiler_params=pltpu.CompilerParams(vmem_limit_bytes=FULL),
        name="weights",
    )(*operands)


def pack_kernel(keep, came, far, far_c, out_h, out, sems):
    width = keep.shape[3] // 3
    tokens = keep.shape[2]
    copies = []
    for y in range(keep.shape[0]):
        for slot in range(2):
            rows = slice(slot * tokens, (slot + 1) * tokens)
            out[y, rows, :width] = keep[y, slot, :, :width]
            out[y, rows, width:2 * width] = came[y, slot, :, :width]
            kv = keep[y, slot, :, width:].astype(jnp.float32) + came[y, slot, :, width:].astype(jnp.float32)
            out[y, rows, 2 * width:] = kv.astype(jnp.bfloat16)
        out[y, 2 * tokens:, :2 * width] = far[...]
        out[y, 2 * tokens:, 2 * width:] = far_c[...]
        copies.append(pltpu.make_async_copy(out.at[y], out_h.at[y], sems.at[y]))
        copies[-1].start()
    for copy in copies:
        copy.wait()


def pack(keep, came, far, far_c):
    y, slots, tokens, lanes = keep.shape
    packed = (y, slots * tokens + far.shape[0], lanes * 4 // 3)
    return pl.pallas_call(
        pack_kernel,
        out_shape=jax.ShapeDtypeStruct(packed, jnp.bfloat16),
        in_specs=[VM] * 4,
        out_specs=HB,
        scratch_shapes=[pltpu.VMEM(packed, jnp.bfloat16), pltpu.SemaphoreType.DMA((y,))],
        compiler_params=pltpu.CompilerParams(vmem_limit_bytes=12 * 2**20),
        name="pack",
    )(keep, came, far, far_c)


def project_kernel(spot, moved, wq, wq_c, out, kv_out, *, slot):
    sources = moved.shape[0]
    groups, tokens, part = out.shape
    width = wq.shape[2]
    size = part // 4
    model = groups * part
    f32 = jnp.float32
    rows = slice(slot * tokens, (slot + 1) * tokens)
    far_rows = slice(2 * tokens, 2 * tokens + size)
    kv_out[...] = summed(moved[:, rows, 2 * width:]).astype(jnp.bfloat16)
    sums = kv_out[...]
    left = jnp.concatenate([moved[s, rows, :2 * width] for s in range(sources)], axis=1)
    first, low = spot[1] == 0, spot[0] == 0

    def kv_term(k_part, v_part):
        rhs = jnp.concatenate([k_part, v_part], axis=1)
        return lax.dot_general(sums, rhs, NT, preferred_element_type=f32)

    def pair(a, b):
        return jnp.concatenate([jnp.where(first, a, b), jnp.where(first, b, a)], axis=1)

    for j in range(groups):
        cols = slice(j * part, (j + 1) * part)
        right = []
        for s in range(sources):
            right += [wq[s, cols, :], wq_c[s, cols, :]]
        acc = lax.dot_general(left, jnp.concatenate(right, axis=1), NT, preferred_element_type=f32)
        near = pair(*[kv_term(w[j, model:model + size, :], w[j, model + size:, :]) for w in (wq, wq_c)])
        far = pair(
            *[
                kv_term(moved[j, far_rows, c:c + width], moved[j, far_rows, c + width:c + 2 * width])
                for c in (0, 2 * width)
            ]
        )
        term = jnp.concatenate([jnp.where(low, near, far), jnp.where(low, far, near)], axis=1)
        out[j] = (acc + term).astype(jnp.bfloat16)


def project(spot, slot, moved, wq, wq_c, tokens, model):
    sources = moved.shape[0]
    width = wq.shape[2]
    groups = 4
    return pl.pallas_call(
        functools.partial(project_kernel, slot=slot),
        out_shape=[
            jax.ShapeDtypeStruct((groups, tokens, model // groups), jnp.bfloat16),
            jax.ShapeDtypeStruct((tokens, 2 * width), jnp.bfloat16),
        ],
        in_specs=[SM] + [VM] * 3,
        out_specs=[VM] * 2,
        compiler_params=pltpu.CompilerParams(vmem_limit_bytes=16 * 2**20),
        cost_estimate=pl.CostEstimate(
            flops=2 * tokens * model * (2 * sources + 2) * width,
            bytes_accessed=8 * 2**20,
            transcendentals=0,
        ),
        name="project",
    )(spot, moved, wq, wq_c)


def summed(terms):
    total = terms[0].astype(jnp.float32)
    for s in range(1, terms.shape[0]):
        total = total + terms[s].astype(jnp.float32)
    return total


def gather_kernel(terms, kv_sum, out):
    part = terms.shape[2]
    out[:, :part] = summed(terms).astype(out.dtype)
    out[:, part:] = kv_sum[...]


def gather(terms, kv_sum):
    cols = terms.shape[2] + kv_sum.shape[1]
    return pl.pallas_call(
        gather_kernel,
        out_shape=jax.ShapeDtypeStruct((terms.shape[1], cols), jnp.bfloat16),
        in_specs=[VM] * 2,
        out_specs=VM,
        compiler_params=pltpu.CompilerParams(vmem_limit_bytes=16 * 2**20),
        name="gather",
    )(terms, kv_sum)


def finish_kernel(terms, kv_sum, far, out, kv_out):
    part = terms.shape[2]
    out[...] = (summed(terms) + far[:, :part].astype(jnp.float32)).astype(out.dtype)
    kv = kv_sum[...].astype(jnp.float32) + far[:, part:].astype(jnp.float32)
    kv_out[...] = kv.astype(kv_out.dtype)


def finish(terms, kv_sum, far):
    return pl.pallas_call(
        finish_kernel,
        out_shape=[
            jax.ShapeDtypeStruct(terms.shape[1:], jnp.bfloat16),
            jax.ShapeDtypeStruct(kv_sum.shape, jnp.bfloat16),
        ],
        in_specs=[VM] * 3,
        out_specs=[VM] * 2,
        compiler_params=pltpu.CompilerParams(vmem_limit_bytes=16 * 2**20),
        name="finish",
    )(terms, kv_sum, far)


def shards(query, query_exp, kv, kv_exp, out_grad, out_grad_exp, q_weight, q_weight_exp, kv_weight, kv_weight_exp):
    swap = [(0, 1), (1, 0)]
    spot = jnp.stack([lax.axis_index("zh"), lax.axis_index("core")]).astype(jnp.int32)
    model = q_weight.shape[0]
    w_all, wkv = weights(q_weight, q_weight_exp, kv_weight, kv_weight_exp, 4)
    w_all = lax.all_to_all(w_all, "y", 0, 0)
    far = lax.ppermute(wkv, "zh", swap)
    keep, send = attention(spot, query, query_exp, kv, kv_exp, out_grad, out_grad_exp)
    came = lax.ppermute(send, "core", swap)
    far_c = lax.ppermute(far, "core", swap)
    packed = pack(keep, came, far, far_c)
    packed, w_all = lax.optimization_barrier((packed, w_all))
    moved = lax.all_to_all(packed, "y", 0, 0)
    w_all_c = lax.ppermute(w_all, "core", swap)
    tokens = keep.shape[2]
    other, kv_other = project(spot, 0, moved, w_all, w_all_c, tokens, model)
    other = lax.all_to_all(other, "x", 0, 0)
    own, kv_own = project(spot, 1, moved, w_all, w_all_c, tokens, model)
    sent = gather(other, kv_other)
    own, sent = lax.optimization_barrier((own, sent))
    far_terms = lax.ppermute(sent, "zh", swap)
    own = lax.all_to_all(own, "x", 0, 0)
    return tuple(finish(own, kv_own, far_terms))


def solution(mesh):
    dp, group, head = (mesh.shape[a] for a in ("dp", "group", "head"))
    fine = Mesh(
        mesh.devices.reshape(dp, group, head // 4, 2, 2), ("dp", "x", "y", "zh", "core")
    )
    head_axes = ("y", "zh", "core")
    columns = P("dp", ("x",) + head_axes)
    exps = P(("x",) + head_axes, "dp")
    tokens = P(("dp",) + head_axes, "x")
    return jax.shard_map(
        shards,
        mesh=fine,
        in_specs=(columns, exps, P("dp", "x"), P("x", "dp"), columns, exps, columns, columns, tokens, tokens),
        out_specs=(tokens, tokens),
        check_vma=False,
    )
```

```python
import functools, math
import jax, jax.numpy as jnp
from jax import lax
from jax.experimental import pallas as pl
from jax.experimental.pallas import tpu as pltpu
from jax.sharding import Mesh, PartitionSpec as P

HB = pl.BlockSpec(memory_space=pltpu.HBM)
VM = pl.BlockSpec(memory_space=pltpu.VMEM)
SM = pl.BlockSpec(memory_space=pltpu.SMEM)
BIG = 58 * 2**20
FULL = 60 * 2**20
NT = (((1,), (1,)), ((), ()))
NN = (((1,), (0,)), ((), ()))


def power(exps):
    return lax.shift_left(jnp.ones_like(exps), exps + 4).astype(jnp.float32) * 0.0625


def fold(x, op):
    rows = x.shape[0]
    while rows > 8:
        rows //= 2
        x = op(x[:rows], x[rows:])
    return x


def attention_kernel(place_s, query_h, q_exp_h, kv_h, kv_exp_h, grad_h, grad_exp_h, keep, send, query, q_exp, kv, kv_exp, grad, grad_exp, out, sems, q_s, k_s, v_s, do_s, kt_s, s_s, dp_s, ds_s, dk_s, dv_s, *, block, tile):
    seq, width = query.shape
    count = seq // block
    blocks = [slice(index * block, (index + 1) * block) for index in range(count)]
    pairs = [(kv_exp_h, kv_exp), (q_exp_h, q_exp), (grad_exp_h, grad_exp), (kv_h, kv)]
    for rows in reversed(blocks):
        pairs += [(query_h.at[rows], query.at[rows]), (grad_h.at[rows], grad.at[rows])]
    loads = [pltpu.make_async_copy(*pair, sems.at[n]) for n, pair in enumerate(pairs)]
    for copy in loads:
        copy.start()
    scale = 1.0 / math.sqrt(width)
    coef = scale * math.log2(math.e)
    for copy in loads[:3]:
        copy.wait()
    exps = jnp.concatenate([q_exp[...], grad_exp[...], kv_exp[...]], axis=0)
    parts = exps.shape[0]
    powers = power(exps).T.astype(jnp.bfloat16)
    row_at = lax.broadcasted_iota(jnp.int32, (parts, parts * 32), 0)
    col_at = lax.broadcasted_iota(jnp.int32, (parts, parts * 32), 1)
    spread = jnp.where(col_at // 32 == row_at, 1.0, 0.0).astype(jnp.bfloat16)

    def scales(rows, low, high):
        return lax.dot_general(
            powers[rows], spread[:, low * width:high * width], NN, preferred_element_type=jnp.float32
        )

    loads[3].wait()
    for rows in blocks:
        both = kv[rows, :].astype(jnp.float32) * scales(rows, 2, 4)
        k_s[rows, :] = both[:, :width].astype(jnp.bfloat16)
        kt_s[:, rows] = both[:, :width].T.astype(jnp.bfloat16)
        v_s[rows, :] = both[:, width:].astype(jnp.bfloat16)

    def fetch(index):
        at = 4 + 2 * (count - 1 - index)
        rows = blocks[index]
        both = scales(rows, 0, 2)
        loads[at].wait()
        q_s[rows, :] = (query[rows, :].astype(jnp.float32) * both[:, :width]).astype(jnp.bfloat16)
        loads[at + 1].wait()
        do_s[rows, :] = (grad[rows, :].astype(jnp.float32) * both[:, width:]).astype(jnp.bfloat16)

    sub = block // tile
    stores = []

    def tiles_of(index):
        return [(t, max(0, t - index * sub) * tile) for t in range((index + 1) * sub)]

    def scores(index, t, low, peak):
        slot = index % 2
        q_b = q_s[index * block + low:(index + 1) * block, :]
        do_b = do_s[index * block + low:(index + 1) * block, :]
        ks = slice(t * tile, (t + 1) * tile)
        s = lax.dot_general(k_s[ks, :], q_b, NT, preferred_element_type=jnp.float32)
        if t >= index * sub:
            key = lax.broadcasted_iota(jnp.int32, (tile, tile), 0)
            row = lax.broadcasted_iota(jnp.int32, (tile, tile), 1)
            head = jnp.where(key <= row, s[:, :tile], -jnp.inf)
            s = jnp.concatenate([head, s[:, tile:]], axis=1) if low + tile < block else head
        s_s[slot, ks, low:] = s
        dp_s[slot, ks, low:] = lax.dot_general(
            v_s[ks, :], do_b, NT, preferred_element_type=jnp.float32
        )
        return merge(peak, fold(s, jnp.maximum), low, jnp.maximum)

    def merge(total, part, low, op):
        if not low:
            return op(total, part)
        return jnp.concatenate([total[:, :low], op(total[:, low:], part)], axis=1)

    lowest = jnp.full((8, block), -jnp.inf, jnp.float32)
    peak = lowest
    fetch(count - 1)
    for t, low in tiles_of(count - 1):
        peak = scores(count - 1, t, low, peak)
    for index in reversed(range(count)):
        first = index * block
        slot = index % 2
        tiles = tiles_of(index)
        peak = jnp.max(peak, axis=0, keepdims=True)
        total = jnp.zeros((8, block), jnp.float32)
        inner = jnp.zeros((8, block), jnp.float32)
        for t, low in tiles:
            ks = slice(t * tile, (t + 1) * tile)
            e = jnp.exp2((s_s[slot, ks, low:] - peak[:, low:]) * coef)
            s_s[slot, ks, low:] = e
            total = merge(total, fold(e, jnp.add), low, jnp.add)
            inner = merge(inner, fold(e * dp_s[slot, ks, low:], jnp.add), low, jnp.add)
        norm = 1.0 / jnp.sum(total, axis=0, keepdims=True)
        delta = jnp.sum(inner, axis=0, keepdims=True) * norm
        coming = tiles_of(index - 1) if index else []
        if index:
            fetch(index - 1)
        peak = lowest
        for at in range(max(len(tiles), len(coming))):
            if at < len(coming):
                peak = scores(index - 1, *coming[at], peak)
            if at >= len(tiles):
                continue
            t, low = tiles[at]
            ks = slice(t * tile, (t + 1) * tile)
            q_b = q_s[first + low:first + block, :]
            do_b = do_s[first + low:first + block, :]
            p = s_s[slot, ks, low:] * norm[:, low:]
            pb = p.astype(jnp.bfloat16)
            ds = (p * (dp_s[slot, ks, low:] - delta[:, low:])).astype(jnp.bfloat16)
            if low:
                ds_s[ks, :low] = jnp.zeros((tile, low), jnp.bfloat16)
            ds_s[ks, low:] = ds
            dv = lax.dot_general(pb, do_b, NN, preferred_element_type=jnp.float32)
            dk = lax.dot_general(ds, q_b, NN, preferred_element_type=jnp.float32)
            if index == count - 1:
                dv_s[ks, :] = dv
                dk_s[ks, :] = dk
            else:
                dv_s[ks, :] += dv
                dk_s[ks, :] += dk
        upper = first + block
        dq = lax.dot_general(kt_s[:, :upper], ds_s[:upper, :], NN, preferred_element_type=jnp.float32)
        dq = ((dq * scale).T).astype(jnp.bfloat16)
        dk = (dk_s[first:upper, :] * scale).astype(jnp.bfloat16)
        dv = dv_s[first:upper, :].astype(jnp.bfloat16)
        place(out, place_s, first, jnp.concatenate([dq, dk, dv], axis=1))
        part = block // (4 * out.shape[3])
        for mine, target in ((0, send), (1, keep)):
            rows = slice(index * part, (index + 1) * part)
            stores.append(
                pltpu.make_async_copy(
                    out.at[mine, rows], target.at[rows], sems.at[len(loads) + len(stores)]
                )
            )
            stores[-1].start()
    for copy in stores:
        copy.wait()


def place(out, spot, first, value):
    piece = out.shape[3]
    for j in range(value.shape[0] // piece):
        h = first // piece + j
        y, z, c = h // 4, (h // 2) % 2, h % 2
        mine = jnp.where(spot[1] == c, 1, 0)
        slot = jnp.where(spot[0] == z, 1, 0)
        out[mine, y, slot] = value[j * piece:(j + 1) * piece]


def attention(spot, query, q_exp, kv, kv_exp, grad, grad_exp, block=512, tile=256):
    seq, width = query.shape
    f32, b16 = jnp.float32, jnp.bfloat16
    sent = (4, 2, seq // 16, 3 * width)
    operands = (query, q_exp, kv, kv_exp, grad, grad_exp)
    return pl.pallas_call(
        functools.partial(attention_kernel, block=block, tile=tile),
        out_shape=[jax.ShapeDtypeStruct(sent, b16)] * 2,
        in_specs=[SM] + [HB] * 6,
        out_specs=[HB] * 2,
        scratch_shapes=[pltpu.VMEM(a.shape, a.dtype) for a in operands]
        + [
            pltpu.VMEM((2,) + sent, b16),
            pltpu.SemaphoreType.DMA((4 + 4 * (seq // block),)),
            pltpu.VMEM((seq, width), b16),
            pltpu.VMEM((seq, width), b16),
            pltpu.VMEM((seq, width), b16),
            pltpu.VMEM((seq, width), b16),
            pltpu.VMEM((width, seq), b16),
            pltpu.VMEM((2, seq, block), f32),
            pltpu.VMEM((2, seq, block), f32),
            pltpu.VMEM((seq, block), b16),
            pltpu.VMEM((seq, width), f32),
            pltpu.VMEM((seq, width), f32),
        ],
        compiler_params=pltpu.CompilerParams(vmem_limit_bytes=FULL),
        cost_estimate=pl.CostEstimate(
            flops=3 * 10**9, bytes_accessed=6 * 2**20, transcendentals=2 * 10**6
        ),
        name="attention",
    )(spot, *operands)


def scaled(mantissa, exps):
    rows, cols = mantissa.shape
    blocks = mantissa.astype(jnp.float32).reshape(rows // 32, 32, cols)
    return (blocks * power(exps)[:, None, :]).reshape(rows, cols).astype(jnp.bfloat16)


def weights_kernel(wq_h, wq_exp_h, wkv_h, wkv_exp_h, all_h, wq, wq_exp, wkv, wkv_exp, out, sems):
    loads = [
        pltpu.make_async_copy(source, target, sems.at[n])
        for n, (source, target) in enumerate(
            ((wkv_exp_h, wkv_exp), (wkv_h, wkv), (wq_exp_h, wq_exp), (wq_h, wq))
        )
    ]
    for copy in loads:
        copy.start()
    for copy in loads:
        copy.wait()
    rows = wq.shape[0]
    size, lanes = wkv.shape
    kv = scaled(wkv[...], wkv_exp[...])
    out[rows:rows + size, :] = kv[:, :lanes // 2]
    out[rows + size:, :] = kv[:, lanes // 2:]
    out[:rows, :] = scaled(wq[...], wq_exp[...])
    stores = [
        pltpu.make_async_copy(out, all_h.at[n], sems.at[4 + n]) for n in range(all_h.shape[0])
    ]
    for copy in stores:
        copy.start()
    for copy in stores:
        copy.wait()


def weights(wq, wq_exp, wkv, wkv_exp, copies):
    operands = (wq, wq_exp, wkv, wkv_exp)
    joined = (wq.shape[0] + 2 * wkv.shape[0], wq.shape[1])
    return pl.pallas_call(
        weights_kernel,
        out_shape=jax.ShapeDtypeStruct((copies,) + joined, jnp.bfloat16),
        in_specs=[HB] * 4,
        out_specs=HB,
        scratch_shapes=[pltpu.VMEM(a.shape, a.dtype) for a in operands]
        + [
            pltpu.VMEM(joined, jnp.bfloat16),
            pltpu.SemaphoreType.DMA((4 + copies,)),
        ],
        compiler_params=pltpu.CompilerParams(vmem_limit_bytes=FULL),
        name="weights",
    )(*operands)


def pack_kernel(keep, came, kv_h, dq_h, kv_out, dq_out, sems):
    width = keep.shape[3] // 3
    tokens = keep.shape[2]
    copies = []
    for y in range(keep.shape[0]):
        for slot in range(2):
            rows = slice(slot * tokens, (slot + 1) * tokens)
            kv = keep[y, slot, :, width:].astype(jnp.float32) + came[y, slot, :, width:].astype(jnp.float32)
            kv_out[y, rows, :] = kv.astype(jnp.bfloat16)
            dq_out[y, rows, :width] = keep[y, slot, :, :width]
            dq_out[y, rows, width:] = came[y, slot, :, :width]
        for out, out_h in ((kv_out, kv_h), (dq_out, dq_h)):
            copies.append(pltpu.make_async_copy(out.at[y], out_h.at[y], sems.at[len(copies)]))
            copies[-1].start()
    for copy in copies:
        copy.wait()


def pack(keep, came):
    y, slots, tokens, lanes = keep.shape
    packed = (y, slots * tokens, lanes * 2 // 3)
    return pl.pallas_call(
        pack_kernel,
        out_shape=[jax.ShapeDtypeStruct(packed, jnp.bfloat16)] * 2,
        in_specs=[VM] * 2,
        out_specs=[HB] * 2,
        scratch_shapes=[pltpu.VMEM(packed, jnp.bfloat16)] * 2
        + [pltpu.SemaphoreType.DMA((2 * y,))],
        compiler_params=pltpu.CompilerParams(vmem_limit_bytes=12 * 2**20),
        name="pack",
    )(keep, came)


def partial_kernel(moved, out):
    out[...] = summed(moved).astype(out.dtype)


def partial_sums(moved):
    return pl.pallas_call(
        partial_kernel,
        out_shape=jax.ShapeDtypeStruct(moved.shape[1:], jnp.bfloat16),
        in_specs=[VM],
        out_specs=VM,
        compiler_params=pltpu.CompilerParams(vmem_limit_bytes=12 * 2**20),
        name="partial",
    )(moved)


def project_kernel(moved, wq, wq_c, out, *, slot):
    sources = moved.shape[0]
    groups, tokens, part = out.shape
    rows = slice(slot * tokens, (slot + 1) * tokens)
    left = jnp.concatenate([moved[s, rows, :] for s in range(sources)], axis=1)
    for j in range(groups):
        cols = slice(j * part, (j + 1) * part)
        right = []
        for s in range(sources):
            right += [wq[s, cols, :], wq_c[s, cols, :]]
        out[j] = lax.dot_general(
            left, jnp.concatenate(right, axis=1), NT, preferred_element_type=jnp.float32
        )


def project(slot, moved, wq, wq_c, tokens, model):
    sources = moved.shape[0]
    width = wq.shape[2]
    groups = 4
    return pl.pallas_call(
        functools.partial(project_kernel, slot=slot),
        out_shape=jax.ShapeDtypeStruct((groups, tokens, model // groups), jnp.float32),
        in_specs=[VM] * 3,
        out_specs=VM,
        compiler_params=pltpu.CompilerParams(vmem_limit_bytes=16 * 2**20),
        cost_estimate=pl.CostEstimate(
            flops=2 * tokens * model * 2 * sources * width,
            bytes_accessed=6 * 2**20,
            transcendentals=0,
        ),
        name="project",
    )(moved, wq, wq_c)


def complete_kernel(spot, acc, part, far, wq, wq_c, out, kv_out, *, slot):
    groups, tokens, size = acc.shape
    rows = slice(slot * tokens, (slot + 1) * tokens)
    far_rows = slice((1 - slot) * tokens, (2 - slot) * tokens)
    kv = part[rows, :].astype(jnp.float32) + far[far_rows, :].astype(jnp.float32)
    kv_out[...] = kv.astype(kv_out.dtype)
    sums = kv_out[...]
    model = groups * size
    piece = size // 4
    first, low = spot[1] == 0, spot[0] == 0
    half = size // 2
    for j in range(groups):
        terms = []
        for w in (wq, wq_c):
            rhs = jnp.concatenate(
                [w[j, model:model + piece, :], w[j, model + piece:, :]], axis=1
            )
            terms.append(lax.dot_general(sums, rhs, NT, preferred_element_type=jnp.float32))
        near = jnp.concatenate(
            [jnp.where(first, *terms), jnp.where(first, *terms[::-1])], axis=1
        )
        none = jnp.zeros_like(near)
        out[j, :, :half] = (acc[j, :, :half] + jnp.where(low, near, none)).astype(out.dtype)
        out[j, :, half:] = (acc[j, :, half:] + jnp.where(low, none, near)).astype(out.dtype)


def complete(spot, slot, acc, part, far, wq, wq_c):
    return pl.pallas_call(
        functools.partial(complete_kernel, slot=slot),
        out_shape=[
            jax.ShapeDtypeStruct(acc.shape, jnp.bfloat16),
            jax.ShapeDtypeStruct((acc.shape[1], part.shape[1]), jnp.bfloat16),
        ],
        in_specs=[SM] + [VM] * 5,
        out_specs=[VM] * 2,
        compiler_params=pltpu.CompilerParams(vmem_limit_bytes=12 * 2**20),
        name="complete",
    )(spot, acc, part, far, wq, wq_c)


def summed(terms):
    total = terms[0].astype(jnp.float32)
    for s in range(1, terms.shape[0]):
        total = total + terms[s].astype(jnp.float32)
    return total


def gather_kernel(terms, out):
    out[...] = summed(terms).astype(out.dtype)


def gather(terms):
    return pl.pallas_call(
        gather_kernel,
        out_shape=jax.ShapeDtypeStruct(terms.shape[1:], jnp.bfloat16),
        in_specs=[VM],
        out_specs=VM,
        compiler_params=pltpu.CompilerParams(vmem_limit_bytes=16 * 2**20),
        name="gather",
    )(terms)


def finish_kernel(terms, far, out):
    out[...] = (summed(terms) + far[...].astype(jnp.float32)).astype(out.dtype)


def finish(terms, far):
    return pl.pallas_call(
        finish_kernel,
        out_shape=jax.ShapeDtypeStruct(terms.shape[1:], jnp.bfloat16),
        in_specs=[VM] * 2,
        out_specs=VM,
        compiler_params=pltpu.CompilerParams(vmem_limit_bytes=16 * 2**20),
        name="finish",
    )(terms, far)


def shards(query, query_exp, kv, kv_exp, out_grad, out_grad_exp, q_weight, q_weight_exp, kv_weight, kv_weight_exp):
    swap = [(0, 1), (1, 0)]
    spot = jnp.stack([lax.axis_index("zh"), lax.axis_index("core")]).astype(jnp.int32)
    model = q_weight.shape[0]
    w_all = lax.all_to_all(
        weights(q_weight, q_weight_exp, kv_weight, kv_weight_exp, 4), "y", 0, 0
    )
    keep, send = attention(spot, query, query_exp, kv, kv_exp, out_grad, out_grad_exp)
    tokens = keep.shape[2]
    kv_sent, dq_sent = pack(keep, lax.ppermute(send, "core", swap))
    kv_sent, dq_sent, w_all = lax.optimization_barrier((kv_sent, dq_sent, w_all))
    kv_moved = lax.all_to_all(kv_sent, "y", 0, 0)
    w_all_c = lax.ppermute(w_all, "core", swap)
    kv_moved, dq_sent = lax.optimization_barrier((kv_moved, dq_sent))
    dq_moved = lax.all_to_all(dq_sent, "y", 0, 0)
    part = partial_sums(kv_moved)
    far = lax.ppermute(part, "zh", swap)
    acc = project(0, dq_moved, w_all, w_all_c, tokens, model)
    other, _ = complete(spot, 0, acc, part, far, w_all, w_all_c)
    other = lax.all_to_all(other, "x", 0, 0)
    acc = project(1, dq_moved, w_all, w_all_c, tokens, model)
    own, kv_grad = complete(spot, 1, acc, part, far, w_all, w_all_c)
    sent = gather(other)
    own, sent = lax.optimization_barrier((own, sent))
    far_terms = lax.ppermute(sent, "zh", swap)
    own = lax.all_to_all(own, "x", 0, 0)
    return finish(own, far_terms), kv_grad


def solution(mesh):
    dp, group, head = (mesh.shape[a] for a in ("dp", "group", "head"))
    fine = Mesh(
        mesh.devices.reshape(dp, group, head // 4, 2, 2), ("dp", "x", "y", "zh", "core")
    )
    head_axes = ("y", "zh", "core")
    columns = P("dp", ("x",) + head_axes)
    exps = P(("x",) + head_axes, "dp")
    tokens = P(("dp",) + head_axes, "x")
    return jax.shard_map(
        shards,
        mesh=fine,
        in_specs=(columns, exps, P("dp", "x"), P("x", "dp"), columns, exps, columns, columns, tokens, tokens),
        out_specs=(tokens, tokens),
        check_vma=False,
    )
```

```python
import functools, math
import jax, jax.numpy as jnp
from jax import lax
from jax.experimental import pallas as pl
from jax.experimental.pallas import tpu as pltpu
from jax.sharding import Mesh, PartitionSpec as P

HB = pl.BlockSpec(memory_space=pltpu.HBM)
VM = pl.BlockSpec(memory_space=pltpu.VMEM)
SM = pl.BlockSpec(memory_space=pltpu.SMEM)
BIG = 58 * 2**20
FULL = 60 * 2**20
NT = (((1,), (1,)), ((), ()))
NN = (((1,), (0,)), ((), ()))


def power(exps):
    return lax.shift_left(jnp.ones_like(exps), exps + 4).astype(jnp.float32) * 0.0625


def fold(x, op):
    rows = x.shape[0]
    while rows > 8:
        rows //= 2
        x = op(x[:rows], x[rows:])
    return x


def attention_kernel(place_s, query_h, q_exp_h, kv_h, kv_exp_h, grad_h, grad_exp_h, keep, send, query, q_exp, kv, kv_exp, grad, grad_exp, out, sems, q_s, k_s, v_s, do_s, kt_s, s_s, dp_s, ds_s, dk_s, dv_s, *, block, tile):
    seq, width = query.shape
    count = seq // block
    blocks = [slice(index * block, (index + 1) * block) for index in range(count)]
    pairs = [(kv_exp_h, kv_exp), (q_exp_h, q_exp), (grad_exp_h, grad_exp), (kv_h, kv)]
    for rows in reversed(blocks):
        pairs += [(query_h.at[rows], query.at[rows]), (grad_h.at[rows], grad.at[rows])]
    loads = [pltpu.make_async_copy(*pair, sems.at[n]) for n, pair in enumerate(pairs)]
    for copy in loads:
        copy.start()
    scale = 1.0 / math.sqrt(width)
    coef = scale * math.log2(math.e)
    for copy in loads[:3]:
        copy.wait()
    exps = jnp.concatenate([q_exp[...], grad_exp[...], kv_exp[...]], axis=0)
    parts = exps.shape[0]
    powers = power(exps).T.astype(jnp.bfloat16)
    row_at = lax.broadcasted_iota(jnp.int32, (parts, parts * 32), 0)
    col_at = lax.broadcasted_iota(jnp.int32, (parts, parts * 32), 1)
    spread = jnp.where(col_at // 32 == row_at, 1.0, 0.0).astype(jnp.bfloat16)

    def scales(rows, low, high):
        return lax.dot_general(
            powers[rows], spread[:, low * width:high * width], NN, preferred_element_type=jnp.float32
        )

    loads[3].wait()
    for rows in blocks:
        both = kv[rows, :].astype(jnp.float32) * scales(rows, 2, 4)
        k_s[rows, :] = both[:, :width].astype(jnp.bfloat16)
        kt_s[:, rows] = both[:, :width].T.astype(jnp.bfloat16)
        v_s[rows, :] = both[:, width:].astype(jnp.bfloat16)

    def fetch(index):
        at = 4 + 2 * (count - 1 - index)
        rows = blocks[index]
        both = scales(rows, 0, 2)
        loads[at].wait()
        q_s[rows, :] = (query[rows, :].astype(jnp.float32) * both[:, :width]).astype(jnp.bfloat16)
        loads[at + 1].wait()
        do_s[rows, :] = (grad[rows, :].astype(jnp.float32) * both[:, width:]).astype(jnp.bfloat16)

    sub = block // tile
    stores = []

    def tiles_of(index):
        return [(t, max(0, t - index * sub) * tile) for t in range((index + 1) * sub)]

    def scores(index, t, low, peak):
        slot = index % 2
        q_b = q_s[index * block + low:(index + 1) * block, :]
        do_b = do_s[index * block + low:(index + 1) * block, :]
        ks = slice(t * tile, (t + 1) * tile)
        s = lax.dot_general(k_s[ks, :], q_b, NT, preferred_element_type=jnp.float32)
        if t >= index * sub:
            key = lax.broadcasted_iota(jnp.int32, (tile, tile), 0)
            row = lax.broadcasted_iota(jnp.int32, (tile, tile), 1)
            head = jnp.where(key <= row, s[:, :tile], -jnp.inf)
            s = jnp.concatenate([head, s[:, tile:]], axis=1) if low + tile < block else head
        s_s[slot, ks, low:] = s
        dp_s[slot, ks, low:] = lax.dot_general(
            v_s[ks, :], do_b, NT, preferred_element_type=jnp.float32
        )
        return merge(peak, fold(s, jnp.maximum), low, jnp.maximum)

    def merge(total, part, low, op):
        if not low:
            return op(total, part)
        return jnp.concatenate([total[:, :low], op(total[:, low:], part)], axis=1)

    lowest = jnp.full((8, block), -jnp.inf, jnp.float32)
    peak = lowest
    fetch(count - 1)
    for t, low in tiles_of(count - 1):
        peak = scores(count - 1, t, low, peak)
    for index in reversed(range(count)):
        first = index * block
        slot = index % 2
        tiles = tiles_of(index)
        peak = jnp.max(peak, axis=0, keepdims=True)
        total = jnp.zeros((8, block), jnp.float32)
        inner = jnp.zeros((8, block), jnp.float32)
        for t, low in tiles:
            ks = slice(t * tile, (t + 1) * tile)
            e = jnp.exp2((s_s[slot, ks, low:] - peak[:, low:]) * coef)
            s_s[slot, ks, low:] = e
            total = merge(total, fold(e, jnp.add), low, jnp.add)
            inner = merge(inner, fold(e * dp_s[slot, ks, low:], jnp.add), low, jnp.add)
        norm = 1.0 / jnp.sum(total, axis=0, keepdims=True)
        delta = jnp.sum(inner, axis=0, keepdims=True) * norm
        coming = tiles_of(index - 1) if index else []
        if index:
            fetch(index - 1)
        peak = lowest
        for at in range(max(len(tiles), len(coming))):
            if at < len(coming):
                peak = scores(index - 1, *coming[at], peak)
            if at >= len(tiles):
                continue
            t, low = tiles[at]
            ks = slice(t * tile, (t + 1) * tile)
            q_b = q_s[first + low:first + block, :]
            do_b = do_s[first + low:first + block, :]
            p = s_s[slot, ks, low:] * norm[:, low:]
            pb = p.astype(jnp.bfloat16)
            ds = (p * (dp_s[slot, ks, low:] - delta[:, low:])).astype(jnp.bfloat16)
            if low:
                ds_s[ks, :low] = jnp.zeros((tile, low), jnp.bfloat16)
            ds_s[ks, low:] = ds
            dv = lax.dot_general(pb, do_b, NN, preferred_element_type=jnp.float32)
            dk = lax.dot_general(ds, q_b, NN, preferred_element_type=jnp.float32)
            if index == count - 1:
                dv_s[ks, :] = dv
                dk_s[ks, :] = dk
            else:
                dv_s[ks, :] += dv
                dk_s[ks, :] += dk
        upper = first + block
        dq = lax.dot_general(kt_s[:, :upper], ds_s[:upper, :], NN, preferred_element_type=jnp.float32)
        dq = ((dq * scale).T).astype(jnp.bfloat16)
        dk = (dk_s[first:upper, :] * scale).astype(jnp.bfloat16)
        dv = dv_s[first:upper, :].astype(jnp.bfloat16)
        place(out, place_s, first, jnp.concatenate([dq, dk, dv], axis=1))
        part = block // (4 * out.shape[3])
        for mine, target in ((0, send), (1, keep)):
            rows = slice(index * part, (index + 1) * part)
            stores.append(
                pltpu.make_async_copy(
                    out.at[mine, rows], target.at[rows], sems.at[len(loads) + len(stores)]
                )
            )
            stores[-1].start()
    for copy in stores:
        copy.wait()


def place(out, spot, first, value):
    piece = out.shape[3]
    for j in range(value.shape[0] // piece):
        h = first // piece + j
        y, z, c = h // 4, (h // 2) % 2, h % 2
        mine = jnp.where(spot[0] % 2 == c, 1, 0)
        slot = jnp.where(spot[0] // 2 == z, 1, 0)
        out[mine, y, slot] = value[j * piece:(j + 1) * piece]


def attention(spot, query, q_exp, kv, kv_exp, grad, grad_exp, block=512, tile=256):
    seq, width = query.shape
    f32, b16 = jnp.float32, jnp.bfloat16
    sent = (4, 2, seq // 16, 3 * width)
    operands = (query, q_exp, kv, kv_exp, grad, grad_exp)
    return pl.pallas_call(
        functools.partial(attention_kernel, block=block, tile=tile),
        out_shape=[jax.ShapeDtypeStruct(sent, b16)] * 2,
        in_specs=[SM] + [HB] * 6,
        out_specs=[HB] * 2,
        scratch_shapes=[pltpu.VMEM(a.shape, a.dtype) for a in operands]
        + [
            pltpu.VMEM((2,) + sent, b16),
            pltpu.SemaphoreType.DMA((4 + 4 * (seq // block),)),
            pltpu.VMEM((seq, width), b16),
            pltpu.VMEM((seq, width), b16),
            pltpu.VMEM((seq, width), b16),
            pltpu.VMEM((seq, width), b16),
            pltpu.VMEM((width, seq), b16),
            pltpu.VMEM((2, seq, block), f32),
            pltpu.VMEM((2, seq, block), f32),
            pltpu.VMEM((seq, block), b16),
            pltpu.VMEM((seq, width), f32),
            pltpu.VMEM((seq, width), f32),
        ],
        compiler_params=pltpu.CompilerParams(vmem_limit_bytes=FULL),
        cost_estimate=pl.CostEstimate(
            flops=3 * 10**9, bytes_accessed=6 * 2**20, transcendentals=2 * 10**6
        ),
        name="attention",
    )(spot, *operands)


def scaled(mantissa, exps):
    rows, cols = mantissa.shape
    blocks = mantissa.astype(jnp.float32).reshape(rows // 32, 32, cols)
    return (blocks * power(exps)[:, None, :]).reshape(rows, cols).astype(jnp.bfloat16)


def weights_kernel(wq_h, wq_exp_h, wkv_h, wkv_exp_h, all_h, kv_h, wq, wq_exp, wkv, wkv_exp, out, kv_out, sems, *, steps):
    rows = wq.shape[0] // steps
    blocks = [slice(n * rows, (n + 1) * rows) for n in range(steps)]
    pairs = [(wq_exp_h, wq_exp)] + [(wq_h.at[at], wq.at[at]) for at in blocks]
    pairs += [(wkv_exp_h, wkv_exp), (wkv_h, wkv)]
    loads = [pltpu.make_async_copy(*pair, sems.at[n]) for n, pair in enumerate(pairs)]
    stores = []

    def store(source, target):
        stores.append(pltpu.make_async_copy(source, target, sems.at[len(loads) + len(stores)]))
        stores[-1].start()

    for copy in loads:
        copy.start()
    loads[0].wait()
    for n, at in enumerate(blocks):
        loads[1 + n].wait()
        out[at, :] = scaled(wq[at, :], wq_exp[n * rows // 32:(n + 1) * rows // 32, :])
        for y in range(all_h.shape[0]):
            store(out.at[at], all_h.at[y, at])
    for copy in loads[1 + steps:]:
        copy.wait()
    kv_out[...] = scaled(wkv[...], wkv_exp[...])
    store(kv_out, kv_h)
    for copy in stores:
        copy.wait()


def weights(wq, wq_exp, wkv, wkv_exp, copies, steps=4):
    operands = (wq, wq_exp, wkv, wkv_exp)
    return pl.pallas_call(
        functools.partial(weights_kernel, steps=steps),
        out_shape=[
            jax.ShapeDtypeStruct((copies,) + wq.shape, jnp.bfloat16),
            jax.ShapeDtypeStruct(wkv.shape, jnp.bfloat16),
        ],
        in_specs=[HB] * 4,
        out_specs=[HB] * 2,
        scratch_shapes=[pltpu.VMEM(a.shape, a.dtype) for a in operands]
        + [
            pltpu.VMEM(wq.shape, jnp.bfloat16),
            pltpu.VMEM(wkv.shape, jnp.bfloat16),
            pltpu.SemaphoreType.DMA((4 + steps + copies * steps,)),
        ],
        compiler_params=pltpu.CompilerParams(vmem_limit_bytes=FULL),
        name="weights",
    )(*operands)


def pack_kernel(keep, came, wkv, wkv_c, kv_h, dq_h, kv_out, dq_out, sems):
    width = keep.shape[3] // 3
    tokens = keep.shape[2]
    copies = []
    for y in range(keep.shape[0]):
        for slot in range(2):
            rows = slice(slot * tokens, (slot + 1) * tokens)
            kv = keep[y, slot, :, width:].astype(jnp.float32) + came[y, slot, :, width:].astype(jnp.float32)
            kv_out[y, rows, :] = kv.astype(jnp.bfloat16)
            dq_out[y, rows, :width] = keep[y, slot, :, :width]
            dq_out[y, rows, width:] = came[y, slot, :, :width]
        dq_out[y, 2 * tokens:2 * tokens + wkv.shape[0], :] = wkv[...]
        dq_out[y, 2 * tokens + wkv.shape[0]:, :] = wkv_c[...]
        for out, out_h in ((kv_out, kv_h), (dq_out, dq_h)):
            copies.append(pltpu.make_async_copy(out.at[y], out_h.at[y], sems.at[len(copies)]))
            copies[-1].start()
    for copy in copies:
        copy.wait()


def pack(keep, came, wkv, wkv_c):
    y, slots, tokens, lanes = keep.shape
    sums = (y, slots * tokens, lanes * 2 // 3)
    packed = (y, slots * tokens + 2 * wkv.shape[0], lanes * 2 // 3)
    return pl.pallas_call(
        pack_kernel,
        out_shape=[jax.ShapeDtypeStruct(sums, jnp.bfloat16), jax.ShapeDtypeStruct(packed, jnp.bfloat16)],
        in_specs=[VM] * 4,
        out_specs=[HB] * 2,
        scratch_shapes=[
            pltpu.VMEM(sums, jnp.bfloat16),
            pltpu.VMEM(packed, jnp.bfloat16),
            pltpu.SemaphoreType.DMA((2 * y,)),
        ],
        compiler_params=pltpu.CompilerParams(vmem_limit_bytes=12 * 2**20),
        name="pack",
    )(keep, came, wkv, wkv_c)


def partial_kernel(moved, out):
    out[...] = summed(moved).astype(out.dtype)


def partial_sums(moved):
    return pl.pallas_call(
        partial_kernel,
        out_shape=jax.ShapeDtypeStruct(moved.shape[1:], jnp.bfloat16),
        in_specs=[VM],
        out_specs=VM,
        compiler_params=pltpu.CompilerParams(vmem_limit_bytes=12 * 2**20),
        name="partial",
    )(moved)


def project_kernel(spot, moved, part, far, wq, wq_c, out, kv_out, *, slot):
    sources = moved.shape[0]
    groups, tokens, size = out.shape
    rows = slice(slot * tokens, (slot + 1) * tokens)
    far_rows = slice((1 - slot) * tokens, (2 - slot) * tokens)
    kv = part[rows, :].astype(jnp.float32) + far[far_rows, :].astype(jnp.float32)
    kv_out[...] = kv.astype(kv_out.dtype)
    sums = kv_out[...]
    first, low = spot[0] % 2 == 0, spot[0] < 2
    near_rows = slice(2 * tokens, (2 * tokens + moved.shape[1]) // 2)
    left = jnp.concatenate([moved[s, rows, :] for s in range(sources)], axis=1)
    for j in range(groups):
        cols = slice(j * size, (j + 1) * size)
        right = []
        for s in range(sources):
            right += [wq[s, cols, :], wq_c[s, cols, :]]
        acc = lax.dot_general(
            left, jnp.concatenate(right, axis=1), NT, preferred_element_type=jnp.float32
        )
        terms = [
            lax.dot_general(sums, w, NT, preferred_element_type=jnp.float32)
            for w in (moved[j, near_rows, :], moved[j, near_rows.stop:, :])
        ]
        near = jnp.concatenate(
            [jnp.where(first, *terms), jnp.where(first, *terms[::-1])], axis=1
        )
        none = jnp.zeros_like(near)
        term = jnp.concatenate([jnp.where(low, near, none), jnp.where(low, none, near)], axis=1)
        out[j] = (acc + term).astype(out.dtype)


def project(spot, slot, moved, part, far, wq, wq_c, tokens):
    sources = moved.shape[0]
    model, width = wq.shape[1:]
    groups = 4
    return pl.pallas_call(
        functools.partial(project_kernel, slot=slot),
        out_shape=[
            jax.ShapeDtypeStruct((groups, tokens, model // groups), jnp.bfloat16),
            jax.ShapeDtypeStruct((tokens, part.shape[1]), jnp.bfloat16),
        ],
        in_specs=[SM] + [VM] * 5,
        out_specs=[VM] * 2,
        compiler_params=pltpu.CompilerParams(vmem_limit_bytes=16 * 2**20),
        cost_estimate=pl.CostEstimate(
            flops=2 * tokens * model * (2 * sources + 2) * width,
            bytes_accessed=6 * 2**20,
            transcendentals=0,
        ),
        name="project",
    )(spot, moved, part, far, wq, wq_c)


def head_terms_kernel(moved, wq, wq_c, out, *, slot):
    sources = moved.shape[0]
    groups, tokens, size = out.shape
    rows = slice(slot * tokens, (slot + 1) * tokens)
    left = jnp.concatenate([moved[s, rows, :] for s in range(sources)], axis=1)
    for j in range(groups):
        cols = slice(j * size, (j + 1) * size)
        right = []
        for s in range(sources):
            right += [wq[s, cols, :], wq_c[s, cols, :]]
        out[j] = lax.dot_general(
            left, jnp.concatenate(right, axis=1), NT, preferred_element_type=jnp.float32
        )


def head_terms(slot, moved, wq, wq_c, tokens):
    sources = moved.shape[0]
    model, width = wq.shape[1:]
    groups = 4
    return pl.pallas_call(
        functools.partial(head_terms_kernel, slot=slot),
        out_shape=jax.ShapeDtypeStruct((groups, tokens, model // groups), jnp.float32),
        in_specs=[VM] * 3,
        out_specs=VM,
        compiler_params=pltpu.CompilerParams(vmem_limit_bytes=16 * 2**20),
        cost_estimate=pl.CostEstimate(
            flops=2 * tokens * model * 2 * sources * width,
            bytes_accessed=6 * 2**20,
            transcendentals=0,
        ),
        name="head_terms",
    )(moved, wq, wq_c)


def complete_kernel(spot, acc, moved, part, far, out, *, slot):
    groups, tokens, size = acc.shape
    rows = slice(slot * tokens, (slot + 1) * tokens)
    far_rows = slice((1 - slot) * tokens, (2 - slot) * tokens)
    kv = part[rows, :].astype(jnp.float32) + far[far_rows, :].astype(jnp.float32)
    sums = kv.astype(jnp.bfloat16)
    first, low = spot[0] % 2 == 0, spot[0] < 2
    near_rows = slice(2 * tokens, (2 * tokens + moved.shape[1]) // 2)
    half = size // 2
    for j in range(groups):
        terms = [
            lax.dot_general(sums, w, NT, preferred_element_type=jnp.float32)
            for w in (moved[j, near_rows, :], moved[j, near_rows.stop:, :])
        ]
        near = jnp.concatenate(
            [jnp.where(first, *terms), jnp.where(first, *terms[::-1])], axis=1
        )
        none = jnp.zeros_like(near)
        out[j, :, :half] = (acc[j, :, :half] + jnp.where(low, near, none)).astype(out.dtype)
        out[j, :, half:] = (acc[j, :, half:] + jnp.where(low, none, near)).astype(out.dtype)


def complete(spot, slot, acc, moved, part, far):
    return pl.pallas_call(
        functools.partial(complete_kernel, slot=slot),
        out_shape=jax.ShapeDtypeStruct(acc.shape, jnp.bfloat16),
        in_specs=[SM] + [VM] * 4,
        out_specs=VM,
        compiler_params=pltpu.CompilerParams(vmem_limit_bytes=12 * 2**20),
        name="complete",
    )(spot, acc, moved, part, far)


def summed(terms):
    total = terms[0].astype(jnp.float32)
    for s in range(1, terms.shape[0]):
        total = total + terms[s].astype(jnp.float32)
    return total


def gather_kernel(terms, out):
    out[...] = summed(terms).astype(out.dtype)


def gather(terms):
    return pl.pallas_call(
        gather_kernel,
        out_shape=jax.ShapeDtypeStruct(terms.shape[1:], jnp.bfloat16),
        in_specs=[VM],
        out_specs=VM,
        compiler_params=pltpu.CompilerParams(vmem_limit_bytes=16 * 2**20),
        name="gather",
    )(terms)


def finish_kernel(terms, far, out):
    out[...] = (summed(terms) + far[...]).astype(out.dtype)


def finish(terms, far):
    return pl.pallas_call(
        finish_kernel,
        out_shape=jax.ShapeDtypeStruct(terms.shape[1:], jnp.bfloat16),
        in_specs=[VM] * 2,
        out_specs=VM,
        compiler_params=pltpu.CompilerParams(vmem_limit_bytes=16 * 2**20),
        name="finish",
    )(terms, far)


def widen_kernel(far, out):
    out[...] = far[...].astype(out.dtype)


def widen(far):
    return pl.pallas_call(
        widen_kernel,
        out_shape=jax.ShapeDtypeStruct(far.shape, jnp.float32),
        in_specs=[VM],
        out_specs=VM,
        compiler_params=pltpu.CompilerParams(vmem_limit_bytes=16 * 2**20),
        cost_estimate=pl.CostEstimate(flops=2 * 10**10, bytes_accessed=2**20, transcendentals=0),
        name="widen",
    )(far)


def shards(query, query_exp, kv, kv_exp, out_grad, out_grad_exp, q_weight, q_weight_exp, kv_weight, kv_weight_exp):
    swap = [(0, 1), (1, 0)]
    spot = (2 * lax.axis_index("zh") + lax.axis_index("core")).astype(jnp.int32).reshape(1)
    w_sent, wkv = weights(q_weight, q_weight_exp, kv_weight, kv_weight_exp, 4)
    w_all = lax.all_to_all(w_sent, "y", 0, 0)
    keep, send = attention(spot, query, query_exp, kv, kv_exp, out_grad, out_grad_exp)
    tokens = keep.shape[2]
    kv_sent, dq_sent = pack(keep, lax.ppermute(send, "core", swap), wkv, lax.ppermute(wkv, "core", swap))
    kv_sent, dq_sent, w_all = lax.optimization_barrier((kv_sent, dq_sent, w_all))
    kv_moved = lax.all_to_all(kv_sent, "y", 0, 0)
    kv_moved, dq_sent, w_all = lax.optimization_barrier((kv_moved, dq_sent, w_all))
    w_all_c = lax.ppermute(w_all, "core", swap)
    moved = lax.all_to_all(dq_sent, "y", 0, 0)
    part = partial_sums(kv_moved)
    far = lax.ppermute(part, "zh", swap)
    acc = head_terms(0, moved, w_all, w_all_c, tokens)
    acc, far = lax.optimization_barrier((acc, far))
    other = complete(spot, 0, acc, moved, part, far)
    other = lax.all_to_all(other, "x", 0, 0)
    own, kv_grad = project(spot, 1, moved, part, far, w_all, w_all_c, tokens)
    sent = gather(other)
    own, sent = lax.optimization_barrier((own, sent))
    far_terms = lax.ppermute(sent, "zh", swap)
    own = lax.all_to_all(own, "x", 0, 0)
    return finish(own, widen(far_terms)), kv_grad


def solution(mesh):
    dp, group, head = (mesh.shape[a] for a in ("dp", "group", "head"))
    fine = Mesh(
        mesh.devices.reshape(dp, group, head // 4, 2, 2), ("dp", "x", "y", "zh", "core")
    )
    head_axes = ("y", "zh", "core")
    columns = P("dp", ("x",) + head_axes)
    exps = P(("x",) + head_axes, "dp")
    tokens = P(("dp",) + head_axes, "x")
    return jax.shard_map(
        shards,
        mesh=fine,
        in_specs=(columns, exps, P("dp", "x"), P("x", "dp"), columns, exps, columns, columns, tokens, tokens),
        out_specs=(tokens, tokens),
        check_vma=False,
    )
```
